32 devices in a mesh: groups: 2 (over y), wide: 4 (over z), narrow: 4 (over x, core).
Axes of the slice: x: 2, y: 2, z: 4, core: 2. Of those that a mesh axis runs over, the one named last changes fastest.
Arguments:
- populations: float32 [19, 96, 192, 128], P(None, ('groups', 'wide'), 'narrow'), parts along dimension 1, may hold values from 0.008 to 0.57, as said below
- flags: int32 [96, 192, 128], P(('groups', 'wide'), 'narrow'), parts along dimension 0, may hold values from 0 to 3, as said below
- potential: float32 [24, 48, 32], P(('groups', 'wide'), 'narrow'), parts along dimension 0, may hold values from -6 to 6
- conductivity: float32 [24, 48, 32], P(('groups', 'wide'), 'narrow'), parts along dimension 0, may hold values from 0.5 to 2
- coil_phase: int32 [24, 48, 32], P(('groups', 'wide'), 'narrow'), parts along dimension 0, may hold values from 0 to 2
- phase_table: float32 [3, 4], replicated, may hold values from -4 to 4
- magnetic: float32 [3, 24, 48, 32], P(None, ('groups', 'wide'), 'narrow'), parts along dimension 1, may hold values from -6 to 6
Outputs:
- populations_out: float32 [19, 96, 192, 128], P(None, ('groups', 'wide'), 'narrow'), parts along dimension 1
- potential_out: float32 [24, 48, 32], P(('groups', 'wide'), 'narrow'), parts along dimension 0
- lorentz: float32 [3, 24, 48, 32], P(None, ('groups', 'wide'), 'narrow'), parts along dimension 1
The draws below stay inside these ranges and needn't reach their ends.
There are 2 independent parts, one for each index of `groups`. The reference program is written for one: setup_inputs(seed, part) draws one part's arguments, and reference() takes and returns one part's arrays. A program takes and returns all parts, laid end to end along the dimension named above; an argument that names none is the same for every part. Nothing has to cross between parts.
Inputs may be any that keep to these rules, and one draw needn't show every extreme that they name: flags: 0 fluid, 1 wall, 2 inlet, 3 outlet. `populations`: each population is its lattice weight times a positive factor.
All inputs are finite; a program needn't handle non-finite values.
Results may differ from the reference program's by a relative error of at most 0.00002.
Values sent between devices are 32-bit elements; how exact they have to be, the bound alone decides.
A program may use at most 64 MiB of HBM per device.

```python
import math
import jax
import jax.numpy as jnp

FX = 128
Q = 19
SWEEPS = 2
NY = 192
NZ = 48
KX = 32
KY = 48
KZ = 12


lattice_weights = [1.0 / 3.0] + [1.0 / 18.0] * 6 + [1.0 / 36.0] * 12


def draw_populations(key, part):
    weights = jnp.array(lattice_weights, jnp.float32)[:, None, None, None]
    factor = jax.random.uniform(key, (Q, NZ, NY, FX), jnp.float32, 0.5, 1.5)
    return weights * factor


def draw_flags(key, part):
    rolled = jax.random.randint(key, (NZ, NY, FX), 0, 20)
    return jnp.where(rolled < 16, 0, jnp.where(rolled < 18, 1, jnp.where(rolled < 19, 2, 3))).astype(jnp.int32)


def touch_ends(entries, stream_key, low, largest):
    spot = [jax.random.randint(jax.random.fold_in(stream_key, axis), (), 0, length) for axis, length in enumerate(entries.shape)]
    longest = entries.shape.index(max(entries.shape))
    beside = spot[:longest] + [(spot[longest] + 1) % entries.shape[longest]] + spot[longest + 1:]
    return entries.at[tuple(spot)].set(low).at[tuple(beside)].set(largest)


def steps_of(stream_key, extent, pieces, low, top_value):
    def one(axis_at, parts):
        heights = jax.random.uniform(jax.random.fold_in(jax.random.fold_in(stream_key, 6), axis_at), (parts,), jnp.float32, low / len(pieces), top_value / len(pieces))
        return jnp.repeat(jnp.exp(heights), extent[axis_at] // parts).reshape((-1,) + (1,) * (len(extent) - axis_at - 1))

    gain = one(*pieces[0])
    for cut in pieces[1:]:
        gain = gain * one(*cut)
    return gain


def gaussian(own_key, dims, width, reach, shards=(), kind=jnp.bfloat16):
    entries = jax.random.normal(own_key, dims, jnp.float32) * width
    if len(shards) > 0:
        entries = steps_of(own_key, dims, shards, -0.22, 0.18) * entries
    return jnp.clip(entries, min=-reach, max=reach).astype(kind)


def setup_inputs(seed: int = 0, part: int = 0) -> dict:
    key_list = jax.random.split(jax.random.key(seed), 8)
    own_keys = jax.random.split(jax.random.fold_in(key_list[7], part), 8)
    return {
        "populations": draw_populations(jax.random.fold_in(jax.random.fold_in(key_list[7], part), 71), part),
        "flags": draw_flags(jax.random.fold_in(jax.random.fold_in(key_list[7], part), 71), part),
        "potential": gaussian(own_keys[2], (KZ, KY, KX), 1.0, 6.0, ((0, 4), (1, 4)), jnp.float32),
        "conductivity": jnp.clip(jnp.exp(math.log(2.0) - 1.3862944 * jax.random.uniform(own_keys[3], (KZ, KY, KX), jnp.float32) ** steps_of(own_keys[3], (KZ, KY, KX), ((0, 4), (1, 4)), -0.2, 0.2)), 0.5, 2.0),
        "coil_phase": touch_ends(jax.random.randint(own_keys[4], (KZ, KY, KX), 0, 3), jax.random.fold_in(own_keys[4], 1), 0, 2).astype(jnp.int32),
        "phase_table": gaussian(key_list[5], (3, 4), 1.0, 4.0, (), jnp.float32),
        "magnetic": gaussian(own_keys[6], (3, KZ, KY, KX), 1.0, 6.0, ((1, 4), (2, 4)), jnp.float32),
    }


lattice_dirs = [(0, 0, 0), (1, 0, 0), (-1, 0, 0), (0, 1, 0), (0, -1, 0), (0, 0, 1), (0, 0, -1), (1, 1, 0), (-1, -1, 0), (1, -1, 0), (-1, 1, 0), (1, 0, 1), (-1, 0, -1), (1, 0, -1), (-1, 0, 1), (0, 1, 1), (0, -1, -1), (0, 1, -1), (0, -1, 1)]
opposite_dir = [0, 2, 1, 4, 3, 6, 5, 8, 7, 10, 9, 12, 11, 14, 13, 16, 15, 18, 17]
lattice_weights = [1.0 / 3.0] + [1.0 / 18.0] * 6 + [1.0 / 36.0] * 12
relax_time = 0.8
force_scale = 0.02
inlet_speed = 0.05


def phase_lookup(coil_phase, phase_table, column):
    summed = jnp.zeros(coil_phase.shape, jnp.float32)
    for phase in range(3):
        summed = summed + jnp.where(coil_phase == phase, phase_table[phase, column], jnp.float32(0.0))
    return summed


def jacobi_sweep(padded, source):
    beside_all = padded[2:, 1:-1, 1:-1] + padded[:-2, 1:-1, 1:-1]
    beside_all = beside_all + padded[1:-1, 2:, 1:-1] + padded[1:-1, :-2, 1:-1]
    beside_all = beside_all + padded[1:-1, 1:-1, 2:] + padded[1:-1, 1:-1, :-2]
    return (beside_all + source) / 6.0


def gradients(padded):
    grad_z = (padded[2:, 1:-1, 1:-1] - padded[:-2, 1:-1, 1:-1]) * 0.5
    grad_y = (padded[1:-1, 2:, 1:-1] - padded[1:-1, :-2, 1:-1]) * 0.5
    grad_x = (padded[1:-1, 1:-1, 2:] - padded[1:-1, 1:-1, :-2]) * 0.5
    return grad_x, grad_y, grad_z


def lorentz_from(grad_x, grad_y, grad_z, conductivity, coil_phase, phase_table, magnetic):
    cur_x = conductivity * (phase_lookup(coil_phase, phase_table, 1) - grad_x)
    cur_y = conductivity * (phase_lookup(coil_phase, phase_table, 2) - grad_y)
    cur_z = conductivity * (phase_lookup(coil_phase, phase_table, 3) - grad_z)
    field_x, field_y, field_z = magnetic[0], magnetic[1], magnetic[2]
    return jnp.stack([cur_y * field_z - cur_z * field_y, cur_z * field_x - cur_x * field_z, cur_x * field_y - cur_y * field_x])


def upsample(lorentz):
    grown = jnp.repeat(jnp.repeat(jnp.repeat(lorentz, 4, axis=1), 4, axis=2), 4, axis=3)
    return grown * force_scale


def collide(popul, flags, force):
    density = jnp.sum(popul, axis=0)
    force_x, force_y, force_z = force[0], force[1], force[2]
    mom_x = jnp.zeros_like(density)
    mom_y = jnp.zeros_like(density)
    mom_z = jnp.zeros_like(density)
    for number in range(19):
        step_x, step_y, step_z = lattice_dirs[number]
        if step_x != 0:
            mom_x = mom_x + step_x * popul[number]
        if step_y != 0:
            mom_y = mom_y + step_y * popul[number]
        if step_z != 0:
            mom_z = mom_z + step_z * popul[number]
    vel_x = (mom_x + 0.5 * force_x) / density
    vel_y = (mom_y + 0.5 * force_y) / density
    vel_z = (mom_z + 0.5 * force_z) / density
    speed_sq = vel_x * vel_x + vel_y * vel_y + vel_z * vel_z
    factor = 1.0 - 0.5 / relax_time
    merged = []
    for number in range(19):
        step_x, step_y, step_z = lattice_dirs[number]
        weight = lattice_weights[number]
        along_u = step_x * vel_x + step_y * vel_y + step_z * vel_z
        along_f = step_x * force_x + step_y * force_y + step_z * force_z
        shape_eq = 1.0 + 3.0 * along_u + 4.5 * along_u * along_u - 1.5 * speed_sq
        balanced = weight * density * shape_eq
        forcing = factor * weight * (3.0 * ((step_x - vel_x) * force_x + (step_y - vel_y) * force_y + (step_z - vel_z) * force_z) + 9.0 * along_u * along_f)
        relaxed = popul[number] - (popul[number] - balanced) / relax_time + forcing
        outflow = weight * shape_eq
        along_in = -step_z * inlet_speed
        inflow = jnp.full_like(density, weight * (1.0 + 3.0 * along_in + 4.5 * along_in * along_in - 1.5 * inlet_speed * inlet_speed))
        chosen = jnp.where(flags == 0, relaxed, jnp.where(flags == 2, inflow, jnp.where(flags == 3, outflow, popul[number])))
        merged.append(chosen)
    return jnp.stack(merged)


def bounce_back(post, pulled, open_pad, flags):
    size_z, size_y, size_x = flags.shape
    merged = []
    for number in range(19):
        step_x, step_y, step_z = lattice_dirs[number]
        open_src = open_pad[1 - step_z:1 - step_z + size_z, 1 - step_y:1 - step_y + size_y, 1 - step_x:1 - step_x + size_x]
        read = jnp.where(open_src == 1, pulled[number], post[opposite_dir[number]])
        merged.append(jnp.where(flags == 1, post[number], read))
    return jnp.stack(merged)


def pull_padded(post_pad, shape):
    size_z, size_y, size_x = shape
    pulled = []
    for number in range(19):
        step_x, step_y, step_z = lattice_dirs[number]
        pulled.append(post_pad[number, 1 - step_z:1 - step_z + size_z, 1 - step_y:1 - step_y + size_y, 1 - step_x:1 - step_x + size_x])
    return pulled


def reference(populations, flags, potential, conductivity, coil_phase, phase_table, magnetic):
    source = conductivity * phase_lookup(coil_phase, phase_table, 0)
    potential_now = potential
    for counter in range(SWEEPS):
        potential_now = jacobi_sweep(jnp.pad(potential_now, 1), source)
    grad_x, grad_y, grad_z = gradients(jnp.pad(potential_now, 1))
    lorentz = lorentz_from(grad_x, grad_y, grad_z, conductivity, coil_phase, phase_table, magnetic)
    force = upsample(lorentz)
    post = collide(populations, flags, force)
    open_cells = (flags != 1).astype(jnp.int32)
    open_pad = jnp.pad(open_cells, 1)
    post_pad = jnp.pad(post, ((0, 0), (1, 1), (1, 1), (1, 1)))
    pulled = pull_padded(post_pad, flags.shape)
    result = bounce_back(post, pulled, open_pad, flags)
    return result, potential_now, lorentz
```

```python
import functools

import jax
import jax.numpy as jnp
from jax import lax
from jax.experimental import pallas as pl
from jax.experimental.pallas import tpu as pltpu
from jax.sharding import PartitionSpec as P

SWEEPS = 2
REACH = 3
SIDE = 8

lattice_dirs = [
    (0, 0, 0),
    (1, 0, 0),
    (-1, 0, 0),
    (0, 1, 0),
    (0, -1, 0),
    (0, 0, 1),
    (0, 0, -1),
    (1, 1, 0),
    (-1, -1, 0),
    (1, -1, 0),
    (-1, 1, 0),
    (1, 0, 1),
    (-1, 0, -1),
    (1, 0, -1),
    (-1, 0, 1),
    (0, 1, 1),
    (0, -1, -1),
    (0, 1, -1),
    (0, -1, 1),
]
opposite_dir = [0, 2, 1, 4, 3, 6, 5, 8, 7, 10, 9, 12, 11, 14, 13, 16, 15, 18, 17]
lattice_weights = [1.0 / 3.0] + [1.0 / 18.0] * 6 + [1.0 / 36.0] * 12
relax_time = 0.8
force_scale = 0.02
inlet_speed = 0.05

flat = [i for i in range(19) if lattice_dirs[i][2] == 0]
rising = [i for i in range(19) if lattice_dirs[i][2] == 1]
sinking = [i for i in range(19) if lattice_dirs[i][2] == -1]
slot_of = {number: place for place, number in enumerate(flat + rising + sinking)}
leaving_y = {
    1: [i for i in range(19) if lattice_dirs[i][1] == 1],
    -1: [i for i in range(19) if lattice_dirs[i][1] == -1],
}
corner_of = {
    (dz, dy): [i for i in range(19) if lattice_dirs[i] == (0, dy, dz)][0]
    for dz in (-1, 1)
    for dy in (-1, 1)
}
ways = [(1, 0), (-1, 0), (0, 1), (0, -1), (1, 1), (1, -1), (-1, 1), (-1, -1)]


def plus(a, b):
    if a is None:
        return b
    if b is None:
        return a
    return a + b


def signed_sum(steps, parts):
    total = None
    for step, part in zip(steps, parts):
        if step != 0:
            total = plus(total, part if step > 0 else -part)
    return total


def exchange_kernel(
    pop_hbm, flags, pot, cond, coil, mag, table,
    post, opened, pot_out, lor_out,
    popv, coarse, rim, cells, ysend, yrecv, lor_rows, force,
    in_sems, coarse_send, coarse_recv, flag_send, flag_recv, post_send, post_recv,
):
    size_z, size_y, size_x = flags.shape
    rough_z, rough_y, rough_x = pot.shape
    tiles = size_y // 8
    up_z, up_y, up_x = size_z // rough_z, size_y // rough_y, size_x // rough_x
    at_z, at_y = lax.axis_index("wide"), lax.axis_index("narrow")
    num_z, num_y = lax.axis_size("wide"), lax.axis_size("narrow")

    def has(dz, dy):
        inside = None
        for step, place, count in ((dz, at_z, num_z), (dy, at_y, num_y)):
            if step != 0:
                this = place < count - 1 if step > 0 else place > 0
                inside = this if inside is None else jnp.logical_and(inside, this)
        return inside

    def target(dz, dy):
        return {"wide": at_z + dz, "narrow": at_y + dy}

    loads = []
    spans = [(0, 1), (size_z - 1, 1), (1, size_z - 2)]
    for number, (first, count) in enumerate(spans):
        copy = pltpu.make_async_copy(
            pop_hbm.at[:, pl.ds(first, count)], popv.at[:, pl.ds(first, count)], in_sems.at[number]
        )
        copy.start()
        loads.append(copy)

    rim[...] = jnp.zeros(rim.shape, jnp.float32)
    rows_ext = cells.shape[1]
    for layer in (0, size_z + 1):
        cells[layer] = jnp.ones((rows_ext, size_x), jnp.int32)
    for first in (0, SIDE + size_y):
        cells[1 : size_z + 1, first : first + SIDE] = jnp.ones((size_z, SIDE, size_x), jnp.int32)

    barrier = pltpu.get_barrier_semaphore()
    for way in ways:
        @pl.when(has(*way))
        def _(way=way):
            pl.semaphore_signal(
                barrier, inc=1, device_id=target(*way), device_id_type=pl.DeviceIdType.MESH
            )

    coarse[...] = jnp.zeros(coarse.shape, jnp.float32)
    lor_rows[...] = jnp.zeros(lor_rows.shape, jnp.float32)

    def looked_up(column):
        phase = coil[...]
        summed = jnp.zeros(phase.shape, jnp.float32)
        for number in range(3):
            summed = summed + jnp.where(phase == number, table[number, column], jnp.float32(0.0))
        return summed

    lanes3 = lax.broadcasted_iota(jnp.int32, coarse.shape, 2)
    coarse[:, 0:rough_y, 0:rough_x] = cond[...] * looked_up(0)
    moved = pltpu.roll(coarse[...], rough_x, 2)
    coarse[:, 0:rough_y, 0:rough_x] = pot[...]
    coarse[...] = jnp.where(lanes3 < rough_x, coarse[...], moved)

    def rough_copy(number):
        dz, dy = ways[number]
        layers = {0: (0, rough_z), 1: (rough_z - 2, 2), -1: (0, 2)}[dz] if dy != 0 else (0, rough_z)
        rows = {0: (0, 16), 1: (8, 8), -1: (0, 8)}[dy]
        return pltpu.make_async_remote_copy(
            src_ref=coarse.at[pl.ds(*layers), pl.ds(*rows)],
            dst_ref=rim.at[number, pl.ds(*layers), pl.ds(0, rows[1])],
            send_sem=coarse_send.at[number],
            recv_sem=coarse_recv.at[number],
            device_id=target(dz, dy),
            device_id_type=pl.DeviceIdType.MESH,
        )

    def flag_copy(number):
        dz, dy = ways[number]
        src_z = {0: (0, size_z), 1: (size_z - 1, 1), -1: (0, 1)}[dz]
        dst_z = {0: 1, 1: 0, -1: size_z + 1}[dz]
        src_y = {0: (0, size_y), 1: (size_y - SIDE, SIDE), -1: (0, SIDE)}[dy]
        dst_y = {0: SIDE, 1: 0, -1: SIDE + size_y}[dy]
        return pltpu.make_async_remote_copy(
            src_ref=flags.at[pl.ds(*src_z), pl.ds(*src_y)],
            dst_ref=cells.at[pl.ds(dst_z, src_z[1]), pl.ds(dst_y, src_y[1])],
            send_sem=flag_send.at[number],
            recv_sem=flag_recv.at[number],
            device_id=target(dz, dy),
            device_id_type=pl.DeviceIdType.MESH,
        )

    def post_copy(number):
        dz, dy = ways[number]
        if dz == 0:
            side = 0 if dy > 0 else 1
            src, dst = ysend.at[side], yrecv.at[side]
        else:
            src_layer = size_z if dz > 0 else 1
            dst_layer = 0 if dz > 0 else size_z + 1
            if dy == 0:
                group = rising if dz > 0 else sinking
                held = pl.ds(slot_of[group[0]], len(group))
                src = post.at[held, src_layer, pl.ds(SIDE, size_y)]
                dst = post.at[held, dst_layer, pl.ds(SIDE, size_y)]
            else:
                slot = slot_of[corner_of[(dz, dy)]]
                src_row, dst_row = (size_y, 0) if dy > 0 else (SIDE, SIDE + size_y)
                src = post.at[slot, src_layer, pl.ds(src_row, SIDE)]
                dst = post.at[slot, dst_layer, pl.ds(dst_row, SIDE)]
        return pltpu.make_async_remote_copy(
            src_ref=src,
            dst_ref=dst,
            send_sem=post_send.at[number],
            recv_sem=post_recv.at[number],
            device_id=target(dz, dy),
            device_id_type=pl.DeviceIdType.MESH,
        )

    def start(make, number):
        @pl.when(has(*ways[number]))
        def _():
            make(number).start()

    def wait_sent(make, number):
        @pl.when(has(*ways[number]))
        def _():
            make(number).wait_send()

    def wait_received(make, number):
        dz, dy = ways[number]

        @pl.when(has(-dz, -dy))
        def _():
            make(number).wait_recv()

    beside_z = (at_z > 0).astype(jnp.int32) + (at_z < num_z - 1).astype(jnp.int32)
    beside_y = (at_y > 0).astype(jnp.int32) + (at_y < num_y - 1).astype(jnp.int32)
    pl.semaphore_wait(barrier, (beside_z + 1) * (beside_y + 1) - 1)

    for number in range(8):
        start(rough_copy, number)
    for number in range(8):
        start(flag_copy, number)

    cells[1 : size_z + 1, SIDE : SIDE + size_y] = flags[...]

    for number in range(8):
        wait_received(rough_copy, number)

    tall = 3 * 8
    row = lax.broadcasted_iota(jnp.int32, (tall, 128), 0)
    lane = lax.broadcasted_iota(jnp.int32, (tall, 128), 1)
    sub = lax.broadcasted_iota(jnp.int32, (8, 128), 0)
    row_all = at_y * rough_y + row - 8
    shown = (lane < rough_x) & (row_all >= 0) & (row_all < num_y * rough_y)
    blocks = {}
    number_of = {way: number for number, way in enumerate(ways)}
    gap = 16 - rough_y
    for dz in (-1, 0, 1):
        for layer in range(rough_z):
            if dz == 0:
                low, high = coarse[layer, 0:8], coarse[layer, 8:16]
            else:
                middle = number_of[(-dz, 0)]
                low, high = rim[middle, layer, 0:8], rim[middle, layer, 8:16]
            before = rim[number_of[(-dz, 1)], layer, 0:8]
            after = rim[number_of[(-dz, -1)], layer, 0:8]
            before = pltpu.roll(before, gap, 0)
            after = jnp.where(sub < rough_y - 8, high, pltpu.roll(after, rough_y - 8, 0))
            blocks[dz * rough_z + layer] = jnp.concatenate([before, low, after], axis=0)
    places = list(range(-REACH, rough_z + REACH))
    field = {p: jnp.where(shown, blocks[p], 0.0) for p in places}
    layer_all = {p: at_z * rough_z + p for p in places}

    def around(v):
        return (
            pltpu.roll(v, 1, 0), pltpu.roll(v, tall - 1, 0), pltpu.roll(v, 1, 1), pltpu.roll(v, 127, 1)
        )

    for sweep in range(SWEEPS):
        fresh = {}
        for p in places[sweep + 1 : len(places) - sweep - 1]:
            back_y, next_y, back_x, next_x = around(field[p])
            source = pltpu.roll(blocks[p], 128 - rough_x, 1)
            total = field[p + 1] + field[p - 1] + next_y + back_y + next_x + back_x + source
            inside = shown & (layer_all[p] >= 0) & (layer_all[p] < num_z * rough_z)
            fresh[p] = jnp.where(inside, total * jnp.float32(1.0 / 6.0), 0.0)
        field = fresh
    held_phase = [looked_up(1 + a) for a in range(3)]
    for layer in range(rough_z):
        back_y, next_y, back_x, next_x = around(field[layer])
        grads = (
            (next_x - back_x) * 0.5, (next_y - back_y) * 0.5, (field[layer + 1] - field[layer - 1]) * 0.5
        )
        pot_out[layer] = field[layer][8 : 8 + rough_y, 0:rough_x]
        cur = [
            cond[layer] * (held_phase[a][layer] - grads[a][8 : 8 + rough_y, 0:rough_x])
            for a in range(3)
        ]
        for a in range(3):
            b, c = (a + 1) % 3, (a + 2) % 3
            value = cur[b] * mag[c, layer] - cur[c] * mag[b, layer]
            lor_out[a, layer] = value
            lor_rows[a * rough_z + layer, 0:rough_y, 0:rough_x] = value

    spread_from = lax.broadcasted_iota(jnp.int32, (128, size_x), 0)
    spread_to = lax.broadcasted_iota(jnp.int32, (128, size_x), 1)
    first_lane = spread_from * up_x
    spread = ((spread_to >= first_lane) & (spread_to < first_lane + up_x)).astype(jnp.float32)
    wide_rows = jnp.dot(
        lor_rows[...].reshape(3 * rough_z * 16, 128),
        spread,
        precision=lax.Precision.HIGHEST,
        preferred_element_type=jnp.float32,
    ) * force_scale
    wide_sub = lax.broadcasted_iota(jnp.int32, (8, size_x), 0)
    for place in range(3 * rough_z):
        for tile in range(tiles):
            value = None
            for part in range(8 // up_y):
                at = place * 16 + tile * (8 // up_y) + part
                line = jnp.broadcast_to(wide_rows[at : at + 1], (8, size_x))
                value = line if value is None else jnp.where(wide_sub < part * up_y, value, line)
            force[place // rough_z, place % rough_z, tile * 8 : tile * 8 + 8] = value

    share = 1.0 - 0.5 / relax_time
    keep = 1.0 - 1.0 / relax_time

    def block(at, first, edge):
        rows = pl.ds(first, 8)
        out_rows = pl.ds(first + SIDE, 8)
        f = [popv[i, at, rows] for i in range(19)]
        kind = flags[at, rows]
        forces = [force[a, lax.div(at, up_z), rows] for a in range(3)]
        fluid = kind == 0
        wall = kind == 1
        inlet = kind == 2
        density = f[0]
        mom = [None, None, None]
        for i in range(1, 19, 2):
            both = f[i] + f[i + 1]
            apart = f[i] - f[i + 1]
            density = density + both
            for a in range(3):
                step = lattice_dirs[i][a]
                if step != 0:
                    part = apart if step > 0 else -apart
                    mom[a] = part if mom[a] is None else (
                        mom[a] + apart if step > 0 else mom[a] - apart
                    )
        inverse = 1.0 / density
        still = (0.0, 0.0, -inlet_speed)
        vel = [
            jnp.where(inlet, jnp.float32(still[a]), (mom[a] + 0.5 * forces[a]) * inverse)
            for a in range(3)
        ]
        scale = jnp.where(fluid, density * (1.0 / relax_time), jnp.where(wall, 0.0, 1.0))
        kept = jnp.where(fluid, jnp.float32(keep), jnp.where(wall, 1.0, 0.0))
        push = [jnp.where(fluid, (3.0 * share) * forces[a], 0.0) for a in range(3)]
        square = vel[0] * vel[0] + vel[1] * vel[1] + vel[2] * vel[2]
        work = vel[0] * push[0] + vel[1] * push[1] + vel[2] * push[2]
        base = scale - (1.5 * scale) * square - work
        scale3 = 3.0 * scale
        result = [None] * 19
        result[0] = kept * f[0] + lattice_weights[0] * base
        based = {w: w * base for w in set(lattice_weights[1:])}
        for i in range(1, 19, 2):
            w = lattice_weights[i]
            along_u = signed_sum(lattice_dirs[i], vel)
            along_f = signed_sum(lattice_dirs[i], push)
            odd = scale3 * along_u + along_f
            even = based[w] + (1.5 * w) * along_u * (odd + along_f)
            odd = w * odd
            one, two = kept * f[i], kept * f[i + 1]
            one, two = jnp.where(wall, two, one), jnp.where(wall, one, two)
            result[i] = one + (even + odd)
            result[i + 1] = two + (even - odd)
        for i in range(19):
            post[slot_of[i], at + 1, out_rows] = result[i]
        if edge != 0:
            side, pick = (0, 7) if edge > 0 else (1, 0)
            for k, i in enumerate(leaving_y[edge]):
                ysend[side, k, pl.ds(at, 1)] = result[i][pick : pick + 1]

    last = size_y - 8
    loads[0].wait()
    loads[1].wait()

    def ends(turn, carry):
        at = turn * (size_z - 1)
        block(at, 0, -1)
        for tile in range(1, tiles - 1):
            block(at, tile * 8, 0)
        block(at, last, 1)
        return carry

    lax.fori_loop(0, 2, ends, 0)
    for number, way in enumerate(ways):
        if way[0] != 0:
            start(post_copy, number)
    loads[2].wait()

    def sides(at, carry):
        block(at, 0, -1)
        block(at, last, 1)
        return carry

    lax.fori_loop(1, size_z - 1, sides, 0)
    for number, way in enumerate(ways):
        if way[0] == 0:
            start(post_copy, number)

    def middles(at, carry):
        for tile in range(1, tiles - 1):
            block(at, tile * 8, 0)
        return carry

    lax.fori_loop(1, size_z - 1, middles, 0)

    for number in range(8):
        wait_received(flag_copy, number)
    end_lane = lax.broadcasted_iota(jnp.int32, (rows_ext, size_x), 1)

    def opens(layer, carry):
        state = jnp.where(cells[layer] != 1, 1, 0)
        opened[1, layer] = state
        opened[2, layer] = jnp.where(end_lane > 0, pltpu.roll(state, 1, 1), 0)
        opened[0, layer] = jnp.where(end_lane < size_x - 1, pltpu.roll(state, size_x - 1, 1), 0)
        return carry

    lax.fori_loop(0, size_z + 2, opens, 0)

    for number in range(8):
        wait_received(post_copy, number)
    for way, row_at in ((1, SIDE - 1), (-1, SIDE + size_y)):
        side = 0 if way > 0 else 1
        for k, i in enumerate(leaving_y[way]):
            for layer in range(size_z):
                post[slot_of[i], layer + 1, row_at : row_at + 1] = yrecv[side, k, layer : layer + 1]

    for number in range(8):
        wait_sent(rough_copy, number)
        wait_sent(flag_copy, number)
        wait_sent(post_copy, number)


def stream_kernel(post, opened, out):
    size_y, size_x = out.shape[2], out.shape[3]
    at = pl.program_id(0) + 1
    own = pl.ds(SIDE, size_y)
    here = opened[1, at, own]
    for i in range(19):
        step_x, step_y, step_z = lattice_dirs[i]
        if i == 0:
            out[0, 0] = post[slot_of[0], at, own]
            continue
        rows = pl.ds(SIDE - step_y, size_y)
        pulled = post[slot_of[i], at - step_z, rows]
        if step_x != 0:
            pulled = pltpu.roll(pulled, step_x % size_x, 1)
        taken = (opened[1 + step_x, at - step_z, rows] & here) != 0
        out[i, 0] = jnp.where(taken, pulled, post[slot_of[opposite_dir[i]], at, own])


def per_device(populations, flags, potential, conductivity, coil_phase, phase_table, magnetic):
    size_z, size_y, size_x = flags.shape
    rough_z, rough_y, rough_x = potential.shape
    assert rough_x * 2 <= 128 and rough_z >= REACH and 11 <= rough_y <= 13
    vmem = pl.BlockSpec(memory_space=pltpu.VMEM)
    ext = (size_z + 2, size_y + 2 * SIDE, size_x)
    f32, i32 = jnp.float32, jnp.int32
    post, opened, potential_now, lorentz = pl.pallas_call(
        exchange_kernel,
        out_shape=(
            pltpu.VMEM((19,) + ext, f32),
            pltpu.VMEM((3,) + ext, i32),
            jax.ShapeDtypeStruct(potential.shape, f32),
            jax.ShapeDtypeStruct(magnetic.shape, f32),
        ),
        in_specs=[pl.BlockSpec(memory_space=pl.ANY)]
        + [vmem] * 5
        + [pl.BlockSpec(memory_space=pltpu.SMEM)],
        out_specs=(vmem,) * 4,
        scratch_shapes=[
            pltpu.VMEM(populations.shape, f32),
            pltpu.VMEM((rough_z, 16, 128), f32),
            pltpu.VMEM((8, rough_z, 16, 128), f32),
            pltpu.VMEM(ext, i32),
            pltpu.VMEM((2, 5, -(-size_z // 8) * 8, size_x), f32),
            pltpu.VMEM((2, 5, -(-size_z // 8) * 8, size_x), f32),
            pltpu.VMEM((3 * rough_z, 16, 128), f32),
            pltpu.VMEM((3, rough_z, size_y, size_x), f32),
            pltpu.SemaphoreType.DMA((3,)),
        ]
        + [pltpu.SemaphoreType.DMA((8,))] * 6,
        compiler_params=pltpu.CompilerParams(
            collective_id=0, has_side_effects=True, vmem_limit_bytes=36 * 2**20
        ),
        name="exchange_and_collide",
    )(populations, flags, potential, conductivity, coil_phase, magnetic, phase_table)
    result = pl.pallas_call(
        stream_kernel,
        grid=(size_z,),
        out_shape=jax.ShapeDtypeStruct(populations.shape, f32),
        in_specs=[vmem, vmem],
        out_specs=pl.BlockSpec((19, 1, size_y, size_x), lambda z: (0, z, 0, 0)),
        compiler_params=pltpu.CompilerParams(vmem_limit_bytes=36 * 2**20),
        name="stream",
    )(post, opened)
    return (result, potential_now, lorentz)


def solution(mesh):
    in_specs = (
        P(None, ("groups", "wide"), "narrow", None),
        P(("groups", "wide"), "narrow", None),
        P(("groups", "wide"), "narrow", None),
        P(("groups", "wide"), "narrow", None),
        P(("groups", "wide"), "narrow", None),
        P(),
        P(None, ("groups", "wide"), "narrow", None),
    )
    out_specs = (
        P(None, ("groups", "wide"), "narrow", None),
        P(("groups", "wide"), "narrow", None),
        P(None, ("groups", "wide"), "narrow", None),
    )
    return jax.shard_map(
        per_device, mesh=mesh, in_specs=in_specs, out_specs=out_specs, check_vma=False
    )
```

```python
import functools

import jax
import jax.numpy as jnp
from jax import lax
from jax.experimental import pallas as pl
from jax.experimental.pallas import tpu as pltpu
from jax.sharding import PartitionSpec as P

SWEEPS = 2
REACH = 3
SIDE = 8

lattice_dirs = [
    (0, 0, 0),
    (1, 0, 0),
    (-1, 0, 0),
    (0, 1, 0),
    (0, -1, 0),
    (0, 0, 1),
    (0, 0, -1),
    (1, 1, 0),
    (-1, -1, 0),
    (1, -1, 0),
    (-1, 1, 0),
    (1, 0, 1),
    (-1, 0, -1),
    (1, 0, -1),
    (-1, 0, 1),
    (0, 1, 1),
    (0, -1, -1),
    (0, 1, -1),
    (0, -1, 1),
]
opposite_dir = [0, 2, 1, 4, 3, 6, 5, 8, 7, 10, 9, 12, 11, 14, 13, 16, 15, 18, 17]
lattice_weights = [1.0 / 3.0] + [1.0 / 18.0] * 6 + [1.0 / 36.0] * 12
relax_time = 0.8
force_scale = 0.02
inlet_speed = 0.05

flat = [i for i in range(19) if lattice_dirs[i][2] == 0]
rising = [i for i in range(19) if lattice_dirs[i][2] == 1]
sinking = [i for i in range(19) if lattice_dirs[i][2] == -1]
slot_of = {number: place for place, number in enumerate(flat + rising + sinking)}
leaving_y = {
    1: [i for i in range(19) if lattice_dirs[i][1] == 1],
    -1: [i for i in range(19) if lattice_dirs[i][1] == -1],
}
corner_of = {
    (dz, dy): [i for i in range(19) if lattice_dirs[i] == (0, dy, dz)][0]
    for dz in (-1, 1)
    for dy in (-1, 1)
}
ways = [(1, 0), (-1, 0), (0, 1), (0, -1), (1, 1), (1, -1), (-1, 1), (-1, -1)]


def plus(a, b):
    if a is None:
        return b
    if b is None:
        return a
    return a + b


def signed_sum(steps, parts):
    total = None
    for step, part in zip(steps, parts):
        if step != 0:
            total = plus(total, part if step > 0 else -part)
    return total


def exchange_kernel(
    pop_hbm, flags_hbm, pot_hbm, cond_hbm, coil_hbm, mag_hbm, table_hbm,
    post, words, pot_out, lor_out,
    popv, pot, cond, coil, mag, table, coarse, rim, cells, bits_x, bits_xy,
    ysend, yrecv, lor_rows, force,
    in_sems, coarse_send, coarse_recv, flag_send, flag_recv, post_send, post_recv,
):
    size_z, size_y, size_x = flags_hbm.shape
    rough_z, rough_y, rough_x = pot.shape
    tiles = size_y // 8
    up_z, up_y, up_x = size_z // rough_z, size_y // rough_y, size_x // rough_x
    at_z, at_y = lax.axis_index("wide"), lax.axis_index("narrow")
    num_z, num_y = lax.axis_size("wide"), lax.axis_size("narrow")

    def has(dz, dy):
        inside = None
        for step, place, count in ((dz, at_z, num_z), (dy, at_y, num_y)):
            if step != 0:
                this = place < count - 1 if step > 0 else place > 0
                inside = this if inside is None else jnp.logical_and(inside, this)
        return inside

    def target(dz, dy):
        return {"wide": at_z + dz, "narrow": at_y + dy}

    smalls = []
    for number, (src, dst) in enumerate(
        [(pot_hbm, pot), (cond_hbm, cond), (coil_hbm, coil), (table_hbm, table),
         (flags_hbm, cells.at[pl.ds(1, size_z), pl.ds(SIDE, size_y)]), (mag_hbm, mag)]
    ):
        copy = pltpu.make_async_copy(src, dst, in_sems.at[3 + number])
        copy.start()
        smalls.append(copy)
    loads = []
    spans = [(0, 1), (size_z - 1, 1), (1, size_z - 2)]
    for number, (first, count) in enumerate(spans):
        copy = pltpu.make_async_copy(
            pop_hbm.at[:, pl.ds(first, count)], popv.at[:, pl.ds(first, count)], in_sems.at[number]
        )
        copy.start()
        loads.append(copy)

    rim[...] = jnp.zeros(rim.shape, jnp.float32)
    rows_ext = cells.shape[1]
    for layer in (0, size_z + 1):
        cells[layer] = jnp.ones((rows_ext, size_x), jnp.int32)
    for first in (0, SIDE + size_y):
        cells[1 : size_z + 1, first : first + SIDE] = jnp.ones((size_z, SIDE, size_x), jnp.int32)

    barrier = pltpu.get_barrier_semaphore()
    for way in ways:
        @pl.when(has(*way))
        def _(way=way):
            pl.semaphore_signal(
                barrier, inc=1, device_id=target(*way), device_id_type=pl.DeviceIdType.MESH
            )

    coarse[...] = jnp.zeros(coarse.shape, jnp.float32)
    lor_rows[...] = jnp.zeros(lor_rows.shape, jnp.float32)

    for copy in smalls[:4]:
        copy.wait()

    def looked_up(column):
        phase = coil[...]
        summed = jnp.zeros(phase.shape, jnp.float32)
        for number in range(3):
            summed = summed + jnp.where(phase == number, table[number : number + 1, column : column + 1], jnp.float32(0.0))
        return summed

    lanes3 = lax.broadcasted_iota(jnp.int32, coarse.shape, 2)
    coarse[:, 0:rough_y, 0:rough_x] = cond[...] * looked_up(0)
    moved = pltpu.roll(coarse[...], rough_x, 2)
    coarse[:, 0:rough_y, 0:rough_x] = pot[...]
    coarse[...] = jnp.where(lanes3 < rough_x, coarse[...], moved)

    def rough_copy(number):
        dz, dy = ways[number]
        layers = {0: (0, rough_z), 1: (rough_z - 2, 2), -1: (0, 2)}[dz] if dy != 0 else (0, rough_z)
        rows = {0: (0, 16), 1: (8, 8), -1: (0, 8)}[dy]
        return pltpu.make_async_remote_copy(
            src_ref=coarse.at[pl.ds(*layers), pl.ds(*rows)],
            dst_ref=rim.at[number, pl.ds(*layers), pl.ds(0, rows[1])],
            send_sem=coarse_send.at[number],
            recv_sem=coarse_recv.at[number],
            device_id=target(dz, dy),
            device_id_type=pl.DeviceIdType.MESH,
        )

    def flag_copy(number):
        dz, dy = ways[number]
        src_z = {0: (0, size_z), 1: (size_z - 1, 1), -1: (0, 1)}[dz]
        dst_z = {0: 1, 1: 0, -1: size_z + 1}[dz]
        src_y = {0: (0, size_y), 1: (size_y - SIDE, SIDE), -1: (0, SIDE)}[dy]
        dst_y = {0: SIDE, 1: 0, -1: SIDE + size_y}[dy]
        return pltpu.make_async_remote_copy(
            src_ref=cells.at[pl.ds(src_z[0] + 1, src_z[1]), pl.ds(src_y[0] + SIDE, src_y[1])],
            dst_ref=cells.at[pl.ds(dst_z, src_z[1]), pl.ds(dst_y, src_y[1])],
            send_sem=flag_send.at[number],
            recv_sem=flag_recv.at[number],
            device_id=target(dz, dy),
            device_id_type=pl.DeviceIdType.MESH,
        )

    def post_copy(number):
        dz, dy = ways[number]
        if dz == 0:
            side = 0 if dy > 0 else 1
            src, dst = ysend.at[side], yrecv.at[side]
        else:
            src_layer = size_z if dz > 0 else 1
            dst_layer = 0 if dz > 0 else size_z + 1
            if dy == 0:
                group = rising if dz > 0 else sinking
                held = pl.ds(slot_of[group[0]], len(group))
                src = post.at[held, src_layer, pl.ds(SIDE, size_y)]
                dst = post.at[held, dst_layer, pl.ds(SIDE, size_y)]
            else:
                slot = slot_of[corner_of[(dz, dy)]]
                src_row, dst_row = (size_y, 0) if dy > 0 else (SIDE, SIDE + size_y)
                src = post.at[slot, src_layer, pl.ds(src_row, SIDE)]
                dst = post.at[slot, dst_layer, pl.ds(dst_row, SIDE)]
        return pltpu.make_async_remote_copy(
            src_ref=src,
            dst_ref=dst,
            send_sem=post_send.at[number],
            recv_sem=post_recv.at[number],
            device_id=target(dz, dy),
            device_id_type=pl.DeviceIdType.MESH,
        )

    def start(make, number):
        @pl.when(has(*ways[number]))
        def _():
            make(number).start()

    def wait_sent(make, number):
        @pl.when(has(*ways[number]))
        def _():
            make(number).wait_send()

    def wait_received(make, number):
        dz, dy = ways[number]

        @pl.when(has(-dz, -dy))
        def _():
            make(number).wait_recv()

    beside_z = (at_z > 0).astype(jnp.int32) + (at_z < num_z - 1).astype(jnp.int32)
    beside_y = (at_y > 0).astype(jnp.int32) + (at_y < num_y - 1).astype(jnp.int32)
    pl.semaphore_wait(barrier, (beside_z + 1) * (beside_y + 1) - 1)

    for number in range(8):
        start(rough_copy, number)
    smalls[4].wait()
    for number in range(8):
        start(flag_copy, number)
    smalls[5].wait()

    for number in range(8):
        wait_received(rough_copy, number)

    tall = 3 * 8
    row = lax.broadcasted_iota(jnp.int32, (tall, 128), 0)
    lane = lax.broadcasted_iota(jnp.int32, (tall, 128), 1)
    sub = lax.broadcasted_iota(jnp.int32, (8, 128), 0)
    row_all = at_y * rough_y + row - 8
    shown = (lane < rough_x) & (row_all >= 0) & (row_all < num_y * rough_y)
    blocks = {}
    number_of = {way: number for number, way in enumerate(ways)}
    gap = 16 - rough_y
    for dz in (-1, 0, 1):
        for layer in range(rough_z):
            if dz == 0:
                low, high = coarse[layer, 0:8], coarse[layer, 8:16]
            else:
                middle = number_of[(-dz, 0)]
                low, high = rim[middle, layer, 0:8], rim[middle, layer, 8:16]
            before = rim[number_of[(-dz, 1)], layer, 0:8]
            after = rim[number_of[(-dz, -1)], layer, 0:8]
            before = pltpu.roll(before, gap, 0)
            after = jnp.where(sub < rough_y - 8, high, pltpu.roll(after, rough_y - 8, 0))
            blocks[dz * rough_z + layer] = jnp.concatenate([before, low, after], axis=0)
    places = list(range(-REACH, rough_z + REACH))
    field = {p: jnp.where(shown, blocks[p], 0.0) for p in places}
    layer_all = {p: at_z * rough_z + p for p in places}

    def around(v):
        return (
            pltpu.roll(v, 1, 0), pltpu.roll(v, tall - 1, 0), pltpu.roll(v, 1, 1), pltpu.roll(v, 127, 1)
        )

    for sweep in range(SWEEPS):
        fresh = {}
        for p in places[sweep + 1 : len(places) - sweep - 1]:
            back_y, next_y, back_x, next_x = around(field[p])
            source = pltpu.roll(blocks[p], 128 - rough_x, 1)
            total = field[p + 1] + field[p - 1] + next_y + back_y + next_x + back_x + source
            inside = shown & (layer_all[p] >= 0) & (layer_all[p] < num_z * rough_z)
            fresh[p] = jnp.where(inside, total * jnp.float32(1.0 / 6.0), 0.0)
        field = fresh
    held_phase = [looked_up(1 + a) for a in range(3)]
    for layer in range(rough_z):
        back_y, next_y, back_x, next_x = around(field[layer])
        grads = (
            (next_x - back_x) * 0.5, (next_y - back_y) * 0.5, (field[layer + 1] - field[layer - 1]) * 0.5
        )
        pot_out[layer] = field[layer][8 : 8 + rough_y, 0:rough_x]
        cur = [
            cond[layer] * (held_phase[a][layer] - grads[a][8 : 8 + rough_y, 0:rough_x])
            for a in range(3)
        ]
        for a in range(3):
            b, c = (a + 1) % 3, (a + 2) % 3
            value = cur[b] * mag[c, layer] - cur[c] * mag[b, layer]
            lor_out[a, layer] = value
            lor_rows[a * rough_z + layer, 0:rough_y, 0:rough_x] = value

    spread_from = lax.broadcasted_iota(jnp.int32, (128, size_x), 0)
    spread_to = lax.broadcasted_iota(jnp.int32, (128, size_x), 1)
    first_lane = spread_from * up_x
    spread = ((spread_to >= first_lane) & (spread_to < first_lane + up_x)).astype(jnp.float32)
    wide_rows = jnp.dot(
        lor_rows[...].reshape(3 * rough_z * 16, 128),
        spread,
        precision=lax.Precision.HIGHEST,
        preferred_element_type=jnp.float32,
    ) * force_scale
    wide_sub = lax.broadcasted_iota(jnp.int32, (8, size_x), 0)
    for place in range(3 * rough_z):
        for tile in range(tiles):
            value = None
            for part in range(8 // up_y):
                at = place * 16 + tile * (8 // up_y) + part
                line = jnp.broadcast_to(wide_rows[at : at + 1], (8, size_x))
                value = line if value is None else jnp.where(wide_sub < part * up_y, value, line)
            force[place // rough_z, place % rough_z, tile * 8 : tile * 8 + 8] = value

    share = 1.0 - 0.5 / relax_time
    keep = 1.0 - 1.0 / relax_time

    def block(at, first, edge):
        rows = pl.ds(first, 8)
        out_rows = pl.ds(first + SIDE, 8)
        f = [popv[i, at, rows] for i in range(19)]
        kind = cells[at + 1, out_rows]
        forces = [force[a, lax.div(at, up_z), rows] for a in range(3)]
        fluid = kind == 0
        wall = kind == 1
        inlet = kind == 2
        density = f[0]
        mom = [None, None, None]
        for i in range(1, 19, 2):
            both = f[i] + f[i + 1]
            apart = f[i] - f[i + 1]
            density = density + both
            for a in range(3):
                step = lattice_dirs[i][a]
                if step != 0:
                    part = apart if step > 0 else -apart
                    mom[a] = part if mom[a] is None else (
                        mom[a] + apart if step > 0 else mom[a] - apart
                    )
        inverse = 1.0 / density
        still = (0.0, 0.0, -inlet_speed)
        vel = [
            jnp.where(inlet, jnp.float32(still[a]), (mom[a] + 0.5 * forces[a]) * inverse)
            for a in range(3)
        ]
        scale = jnp.where(fluid, density * (1.0 / relax_time), jnp.where(wall, 0.0, 1.0))
        kept = jnp.where(fluid, jnp.float32(keep), jnp.where(wall, 1.0, 0.0))
        push = [jnp.where(fluid, (3.0 * share) * forces[a], 0.0) for a in range(3)]
        square = vel[0] * vel[0] + vel[1] * vel[1] + vel[2] * vel[2]
        work = vel[0] * push[0] + vel[1] * push[1] + vel[2] * push[2]
        base = scale - (1.5 * scale) * square - work
        scale3 = 3.0 * scale
        result = [None] * 19
        result[0] = kept * f[0] + lattice_weights[0] * base
        based = {w: w * base for w in set(lattice_weights[1:])}
        for i in range(1, 19, 2):
            w = lattice_weights[i]
            along_u = signed_sum(lattice_dirs[i], vel)
            along_f = signed_sum(lattice_dirs[i], push)
            odd = scale3 * along_u + along_f
            even = based[w] + (1.5 * w) * along_u * (odd + along_f)
            odd = w * odd
            one, two = kept * f[i], kept * f[i + 1]
            one, two = jnp.where(wall, two, one), jnp.where(wall, one, two)
            result[i] = one + (even + odd)
            result[i + 1] = two + (even - odd)
        for i in range(19):
            post[slot_of[i], at + 1, out_rows] = result[i]
        if edge != 0:
            side, pick = (0, 7) if edge > 0 else (1, 0)
            for k, i in enumerate(leaving_y[edge]):
                ysend[side, k, pl.ds(at, 1)] = result[i][pick : pick + 1]

    last = size_y - 8
    loads[0].wait()
    loads[1].wait()

    def ends(turn, carry):
        at = turn * (size_z - 1)
        block(at, 0, -1)
        for tile in range(1, tiles - 1):
            block(at, tile * 8, 0)
        block(at, last, 1)
        return carry

    lax.fori_loop(0, 2, ends, 0)
    for number, way in enumerate(ways):
        if way[0] != 0:
            start(post_copy, number)
    loads[2].wait()

    def sides(at, carry):
        block(at, 0, -1)
        block(at, last, 1)
        return carry

    lax.fori_loop(1, size_z - 1, sides, 0)
    for number, way in enumerate(ways):
        if way[0] == 0:
            start(post_copy, number)

    def middles(at, carry):
        for tile in range(1, tiles - 1):
            block(at, tile * 8, 0)
        return carry

    lax.fori_loop(1, size_z - 1, middles, 0)

    for number in range(8):
        wait_received(flag_copy, number)
    end_lane = lax.broadcasted_iota(jnp.int32, (rows_ext, size_x), 1)

    def opens(layer, carry):
        state = jnp.where(cells[layer] != 1, 1, 0)
        back = jnp.where(end_lane > 0, pltpu.roll(state, 1, 1), 0)
        ahead = jnp.where(end_lane < size_x - 1, pltpu.roll(state, size_x - 1, 1), 0)
        bits_x[...] = state + 2 * back + 4 * ahead
        near = bits_x[SIDE - 1 : SIDE - 1 + size_y], bits_x[SIDE + 1 : SIDE + 1 + size_y]
        bits_xy[layer] = bits_x[SIDE : SIDE + size_y] + 8 * near[0] + 64 * near[1]
        return carry

    lax.fori_loop(0, size_z + 2, opens, 0)

    def join(at, carry):
        here = bits_xy[at + 1]
        word = here + 512 * bits_xy[at] + 262144 * bits_xy[at + 2]
        words[at] = jnp.where((here & 1) != 0, word, 0)
        return carry

    lax.fori_loop(0, size_z, join, 0)

    for number in range(8):
        wait_received(post_copy, number)
    for way, row_at in ((1, SIDE - 1), (-1, SIDE + size_y)):
        side = 0 if way > 0 else 1
        for k, i in enumerate(leaving_y[way]):
            for layer in range(size_z):
                post[slot_of[i], layer + 1, row_at : row_at + 1] = yrecv[side, k, layer : layer + 1]

    for number in range(8):
        wait_sent(rough_copy, number)
        wait_sent(flag_copy, number)
        wait_sent(post_copy, number)


def bit_of(step_x, step_y, step_z):
    place = {0: 0, 1: 1, -1: 2}
    return 1 << (place[step_x] + 3 * place[step_y] + 9 * place[step_z])


def stream_kernel(post, words, pot_in, lor_in, out, pot_out, lor_out, held, sems, small_sems):
    size_z, size_y, size_x = words.shape
    own = pl.ds(SIDE, size_y)
    smalls = [
        pltpu.make_async_copy(pot_in, pot_out, small_sems.at[0]),
        pltpu.make_async_copy(lor_in, lor_out, small_sems.at[1]),
    ]
    for copy in smalls:
        copy.start()

    def store(at):
        return pltpu.make_async_copy(
            held.at[:, pl.ds(at, 1)], out.at[:, pl.ds(at, 1)], sems.at[at]
        )

    def layer(at, carry):
        word = words[at]
        held[0, at] = post[slot_of[0], at + 1, own]
        for i in range(1, 19):
            step_x, step_y, step_z = lattice_dirs[i]
            pulled = post[slot_of[i], at + 1 - step_z, pl.ds(SIDE - step_y, size_y)]
            if step_x != 0:
                pulled = pltpu.roll(pulled, step_x % size_x, 1)
            taken = (word & bit_of(step_x, step_y, step_z)) != 0
            held[i, at] = jnp.where(taken, pulled, post[slot_of[opposite_dir[i]], at + 1, own])
        store(at).start()
        return carry

    lax.fori_loop(0, size_z, layer, 0)

    def finish(at, carry):
        store(at).wait()
        return carry

    lax.fori_loop(0, size_z, finish, 0)
    for copy in smalls:
        copy.wait()


def per_device(populations, flags, potential, conductivity, coil_phase, phase_table, magnetic):
    size_z, size_y, size_x = flags.shape
    rough_z, rough_y, rough_x = potential.shape
    assert rough_x * 2 <= 128 and rough_z >= REACH and 11 <= rough_y <= 13
    vmem = pl.BlockSpec(memory_space=pltpu.VMEM)
    hbm = pl.BlockSpec(memory_space=pltpu.HBM)
    ext = (size_z + 2, size_y + 2 * SIDE, size_x)
    f32, i32 = jnp.float32, jnp.int32
    post, words, potential_now, lorentz = pl.pallas_call(
        exchange_kernel,
        out_shape=(
            pltpu.VMEM((19,) + ext, f32),
            pltpu.VMEM(flags.shape, i32),
            pltpu.VMEM(potential.shape, f32),
            pltpu.VMEM(magnetic.shape, f32),
        ),
        in_specs=[hbm] * 7,
        out_specs=(vmem,) * 4,
        scratch_shapes=[
            pltpu.VMEM(populations.shape, f32),
            pltpu.VMEM(potential.shape, f32),
            pltpu.VMEM(potential.shape, f32),
            pltpu.VMEM(potential.shape, i32),
            pltpu.VMEM(magnetic.shape, f32),
            pltpu.VMEM(phase_table.shape, f32),
            pltpu.VMEM((rough_z, 16, 128), f32),
            pltpu.VMEM((8, rough_z, 16, 128), f32),
            pltpu.VMEM(ext, i32),
            pltpu.VMEM(ext[1:], i32),
            pltpu.VMEM((size_z + 2, size_y, size_x), i32),
            pltpu.VMEM((2, 5, -(-size_z // 8) * 8, size_x), f32),
            pltpu.VMEM((2, 5, -(-size_z // 8) * 8, size_x), f32),
            pltpu.VMEM((3 * rough_z, 16, 128), f32),
            pltpu.VMEM((3, rough_z, size_y, size_x), f32),
            pltpu.SemaphoreType.DMA((9,)),
        ]
        + [pltpu.SemaphoreType.DMA((8,))] * 6,
        compiler_params=pltpu.CompilerParams(
            collective_id=0, has_side_effects=True, vmem_limit_bytes=24 * 2**20
        ),
        name="exchange_and_collide",
    )(
        *(
            pltpu.with_memory_space_constraint(x, pltpu.HBM)
            for x in (
                populations, flags, potential, conductivity, coil_phase, magnetic, phase_table
            )
        )
    )
    result, potential_now, lorentz = pl.pallas_call(
        stream_kernel,
        out_shape=(
            jax.ShapeDtypeStruct(populations.shape, f32),
            jax.ShapeDtypeStruct(potential.shape, f32),
            jax.ShapeDtypeStruct(magnetic.shape, f32),
        ),
        in_specs=[vmem] * 4,
        out_specs=(hbm,) * 3,
        scratch_shapes=[
            pltpu.VMEM(populations.shape, f32),
            pltpu.SemaphoreType.DMA((size_z,)),
            pltpu.SemaphoreType.DMA((2,)),
        ],
        compiler_params=pltpu.CompilerParams(vmem_limit_bytes=24 * 2**20),
        name="stream",
    )(
        *(
            pltpu.with_memory_space_constraint(x, pltpu.VMEM)
            for x in (post, words, potential_now, lorentz)
        )
    )
    return (result, potential_now, lorentz)


def solution(mesh):
    in_specs = (
        P(None, ("groups", "wide"), "narrow", None),
        P(("groups", "wide"), "narrow", None),
        P(("groups", "wide"), "narrow", None),
        P(("groups", "wide"), "narrow", None),
        P(("groups", "wide"), "narrow", None),
        P(),
        P(None, ("groups", "wide"), "narrow", None),
    )
    out_specs = (
        P(None, ("groups", "wide"), "narrow", None),
        P(("groups", "wide"), "narrow", None),
        P(None, ("groups", "wide"), "narrow", None),
    )
    return jax.shard_map(
        per_device, mesh=mesh, in_specs=in_specs, out_specs=out_specs, check_vma=False
    )
```

```python
import functools

import jax
import jax.numpy as jnp
from jax import lax
from jax.experimental import pallas as pl
from jax.experimental.pallas import tpu as pltpu
from jax.sharding import PartitionSpec as P

SWEEPS = 2
REACH = 3
SIDE = 8

lattice_dirs = [
    (0, 0, 0),
    (1, 0, 0),
    (-1, 0, 0),
    (0, 1, 0),
    (0, -1, 0),
    (0, 0, 1),
    (0, 0, -1),
    (1, 1, 0),
    (-1, -1, 0),
    (1, -1, 0),
    (-1, 1, 0),
    (1, 0, 1),
    (-1, 0, -1),
    (1, 0, -1),
    (-1, 0, 1),
    (0, 1, 1),
    (0, -1, -1),
    (0, 1, -1),
    (0, -1, 1),
]
opposite_dir = [0, 2, 1, 4, 3, 6, 5, 8, 7, 10, 9, 12, 11, 14, 13, 16, 15, 18, 17]
lattice_weights = [1.0 / 3.0] + [1.0 / 18.0] * 6 + [1.0 / 36.0] * 12
relax_time = 0.8
force_scale = 0.02
inlet_speed = 0.05

flat = [i for i in range(19) if lattice_dirs[i][2] == 0]
rising = [i for i in range(19) if lattice_dirs[i][2] == 1]
sinking = [i for i in range(19) if lattice_dirs[i][2] == -1]
slot_of = {number: place for place, number in enumerate(flat + rising + sinking)}
leaving_y = {
    1: [i for i in range(19) if lattice_dirs[i][1] == 1],
    -1: [i for i in range(19) if lattice_dirs[i][1] == -1],
}
corner_of = {
    (dz, dy): [i for i in range(19) if lattice_dirs[i] == (0, dy, dz)][0]
    for dz in (-1, 1)
    for dy in (-1, 1)
}
ways = [(1, 0), (-1, 0), (0, 1), (0, -1), (1, 1), (1, -1), (-1, 1), (-1, -1)]


def plus(a, b):
    if a is None:
        return b
    if b is None:
        return a
    return a + b


def signed_sum(steps, parts):
    total = None
    for step, part in zip(steps, parts):
        if step != 0:
            total = plus(total, part if step > 0 else -part)
    return total


def exchange_kernel(
    pop_hbm, flags_hbm, pot_hbm, cond_hbm, coil_hbm, mag_hbm, table_hbm,
    post, words, pot_out, lor_out,
    popv, pot, cond, coil, mag, table, coarse, rim, cells, bits_x, bits_xy,
    ysend, yrecv, lor_rows, force,
    in_sems, coarse_send, coarse_recv, flag_send, flag_recv, post_send, post_recv,
):
    size_z, size_y, size_x = flags_hbm.shape
    rough_z, rough_y, rough_x = pot.shape
    tiles = size_y // 8
    up_z, up_y, up_x = size_z // rough_z, size_y // rough_y, size_x // rough_x
    at_z, at_y = lax.axis_index("wide"), lax.axis_index("narrow")
    num_z, num_y = lax.axis_size("wide"), lax.axis_size("narrow")

    def has(dz, dy):
        inside = None
        for step, place, count in ((dz, at_z, num_z), (dy, at_y, num_y)):
            if step != 0:
                this = place < count - 1 if step > 0 else place > 0
                inside = this if inside is None else jnp.logical_and(inside, this)
        return inside

    def target(dz, dy):
        return {"wide": at_z + dz, "narrow": at_y + dy}

    smalls = []
    for number, (src, dst) in enumerate(
        [(pot_hbm, pot), (cond_hbm, cond), (coil_hbm, coil), (table_hbm, table),
         (flags_hbm, cells.at[pl.ds(1, size_z), pl.ds(SIDE, size_y)]), (mag_hbm, mag)]
    ):
        copy = pltpu.make_async_copy(src, dst, in_sems.at[3 + number])
        copy.start()
        smalls.append(copy)
    loads = []
    spans = [(size_z - 1, 1), (0, 1), (1, size_z - 2)]
    for number, (first, count) in enumerate(spans):
        copy = pltpu.make_async_copy(
            pop_hbm.at[:, pl.ds(first, count)], popv.at[:, pl.ds(first, count)], in_sems.at[number]
        )
        copy.start()
        loads.append(copy)

    rim[...] = jnp.zeros(rim.shape, jnp.float32)
    rows_ext = cells.shape[1]
    for layer in (0, size_z + 1):
        cells[layer] = jnp.ones((rows_ext, size_x), jnp.int32)
    for first in (0, SIDE + size_y):
        cells[1 : size_z + 1, first : first + SIDE] = jnp.ones((size_z, SIDE, size_x), jnp.int32)

    barrier = pltpu.get_barrier_semaphore()
    for way in ways:
        @pl.when(has(*way))
        def _(way=way):
            pl.semaphore_signal(
                barrier, inc=1, device_id=target(*way), device_id_type=pl.DeviceIdType.MESH
            )

    coarse[...] = jnp.zeros(coarse.shape, jnp.float32)
    lor_rows[...] = jnp.zeros(lor_rows.shape, jnp.float32)

    for copy in smalls[:4]:
        copy.wait()

    def looked_up(column):
        phase = coil[...]
        summed = jnp.zeros(phase.shape, jnp.float32)
        for number in range(3):
            summed = summed + jnp.where(phase == number, table[number : number + 1, column : column + 1], jnp.float32(0.0))
        return summed

    lanes3 = lax.broadcasted_iota(jnp.int32, coarse.shape, 2)
    coarse[:, 0:rough_y, 0:rough_x] = cond[...] * looked_up(0)
    moved = pltpu.roll(coarse[...], rough_x, 2)
    coarse[:, 0:rough_y, 0:rough_x] = pot[...]
    coarse[...] = jnp.where(lanes3 < rough_x, coarse[...], moved)

    def rough_copy(number):
        dz, dy = ways[number]
        layers = {0: (0, rough_z), 1: (rough_z - 2, 2), -1: (0, 2)}[dz] if dy != 0 else (0, rough_z)
        rows = {0: (0, 16), 1: (8, 8), -1: (0, 8)}[dy]
        return pltpu.make_async_remote_copy(
            src_ref=coarse.at[pl.ds(*layers), pl.ds(*rows)],
            dst_ref=rim.at[number, pl.ds(*layers), pl.ds(0, rows[1])],
            send_sem=coarse_send.at[number],
            recv_sem=coarse_recv.at[number],
            device_id=target(dz, dy),
            device_id_type=pl.DeviceIdType.MESH,
        )

    def flag_copy(number):
        dz, dy = ways[number]
        src_z = {0: (0, size_z), 1: (size_z - 1, 1), -1: (0, 1)}[dz]
        dst_z = {0: 1, 1: 0, -1: size_z + 1}[dz]
        src_y = {0: (0, size_y), 1: (size_y - SIDE, SIDE), -1: (0, SIDE)}[dy]
        dst_y = {0: SIDE, 1: 0, -1: SIDE + size_y}[dy]
        return pltpu.make_async_remote_copy(
            src_ref=cells.at[pl.ds(src_z[0] + 1, src_z[1]), pl.ds(src_y[0] + SIDE, src_y[1])],
            dst_ref=cells.at[pl.ds(dst_z, src_z[1]), pl.ds(dst_y, src_y[1])],
            send_sem=flag_send.at[number],
            recv_sem=flag_recv.at[number],
            device_id=target(dz, dy),
            device_id_type=pl.DeviceIdType.MESH,
        )

    def post_copy(number):
        dz, dy = ways[number]
        if dz == 0:
            side = 0 if dy > 0 else 1
            src, dst = ysend.at[side], yrecv.at[side]
        else:
            src_layer = size_z if dz > 0 else 1
            dst_layer = 0 if dz > 0 else size_z + 1
            if dy == 0:
                group = rising if dz > 0 else sinking
                held = pl.ds(slot_of[group[0]], len(group))
                src = post.at[held, src_layer, pl.ds(SIDE, size_y)]
                dst = post.at[held, dst_layer, pl.ds(SIDE, size_y)]
            else:
                slot = slot_of[corner_of[(dz, dy)]]
                src_row, dst_row = (size_y, 0) if dy > 0 else (SIDE, SIDE + size_y)
                src = post.at[slot, src_layer, pl.ds(src_row, SIDE)]
                dst = post.at[slot, dst_layer, pl.ds(dst_row, SIDE)]
        return pltpu.make_async_remote_copy(
            src_ref=src,
            dst_ref=dst,
            send_sem=post_send.at[number],
            recv_sem=post_recv.at[number],
            device_id=target(dz, dy),
            device_id_type=pl.DeviceIdType.MESH,
        )

    def start(make, number):
        @pl.when(has(*ways[number]))
        def _():
            make(number).start()

    def wait_sent(make, number):
        @pl.when(has(*ways[number]))
        def _():
            make(number).wait_send()

    def wait_received(make, number):
        dz, dy = ways[number]

        @pl.when(has(-dz, -dy))
        def _():
            make(number).wait_recv()

    beside_z = (at_z > 0).astype(jnp.int32) + (at_z < num_z - 1).astype(jnp.int32)
    beside_y = (at_y > 0).astype(jnp.int32) + (at_y < num_y - 1).astype(jnp.int32)
    pl.semaphore_wait(barrier, (beside_z + 1) * (beside_y + 1) - 1)

    for number in range(8):
        start(rough_copy, number)
    smalls[4].wait()
    for number in range(8):
        start(flag_copy, number)
    smalls[5].wait()

    for number in range(8):
        wait_received(rough_copy, number)

    tall = 3 * 8
    row = lax.broadcasted_iota(jnp.int32, (tall, 128), 0)
    lane = lax.broadcasted_iota(jnp.int32, (tall, 128), 1)
    sub = lax.broadcasted_iota(jnp.int32, (8, 128), 0)
    row_all = at_y * rough_y + row - 8
    shown = (lane < rough_x) & (row_all >= 0) & (row_all < num_y * rough_y)
    blocks = {}
    number_of = {way: number for number, way in enumerate(ways)}
    gap = 16 - rough_y
    for dz in (-1, 0, 1):
        for layer in range(rough_z):
            if dz == 0:
                low, high = coarse[layer, 0:8], coarse[layer, 8:16]
            else:
                middle = number_of[(-dz, 0)]
                low, high = rim[middle, layer, 0:8], rim[middle, layer, 8:16]
            before = rim[number_of[(-dz, 1)], layer, 0:8]
            after = rim[number_of[(-dz, -1)], layer, 0:8]
            before = pltpu.roll(before, gap, 0)
            after = jnp.where(sub < rough_y - 8, high, pltpu.roll(after, rough_y - 8, 0))
            blocks[dz * rough_z + layer] = jnp.concatenate([before, low, after], axis=0)
    places = list(range(-REACH, rough_z + REACH))
    field = {p: jnp.where(shown, blocks[p], 0.0) for p in places}
    layer_all = {p: at_z * rough_z + p for p in places}

    def around(v):
        return (
            pltpu.roll(v, 1, 0), pltpu.roll(v, tall - 1, 0), pltpu.roll(v, 1, 1), pltpu.roll(v, 127, 1)
        )

    for sweep in range(SWEEPS):
        fresh = {}
        for p in places[sweep + 1 : len(places) - sweep - 1]:
            back_y, next_y, back_x, next_x = around(field[p])
            source = pltpu.roll(blocks[p], 128 - rough_x, 1)
            total = field[p + 1] + field[p - 1] + next_y + back_y + next_x + back_x + source
            inside = shown & (layer_all[p] >= 0) & (layer_all[p] < num_z * rough_z)
            fresh[p] = jnp.where(inside, total * jnp.float32(1.0 / 6.0), 0.0)
        field = fresh
    held_phase = [looked_up(1 + a) for a in range(3)]
    for layer in range(rough_z):
        back_y, next_y, back_x, next_x = around(field[layer])
        grads = (
            (next_x - back_x) * 0.5, (next_y - back_y) * 0.5, (field[layer + 1] - field[layer - 1]) * 0.5
        )
        pot_out[layer] = field[layer][8 : 8 + rough_y, 0:rough_x]
        cur = [
            cond[layer] * (held_phase[a][layer] - grads[a][8 : 8 + rough_y, 0:rough_x])
            for a in range(3)
        ]
        for a in range(3):
            b, c = (a + 1) % 3, (a + 2) % 3
            value = cur[b] * mag[c, layer] - cur[c] * mag[b, layer]
            lor_out[a, layer] = value
            lor_rows[a * rough_z + layer, 0:rough_y, 0:rough_x] = value

    spread_from = lax.broadcasted_iota(jnp.int32, (128, size_x), 0)
    spread_to = lax.broadcasted_iota(jnp.int32, (128, size_x), 1)
    first_lane = spread_from * up_x
    spread = ((spread_to >= first_lane) & (spread_to < first_lane + up_x)).astype(jnp.float32)
    wide_rows = jnp.dot(
        lor_rows[...].reshape(3 * rough_z * 16, 128),
        spread,
        precision=lax.Precision.HIGHEST,
        preferred_element_type=jnp.float32,
    ) * (0.5 * force_scale)
    wide_sub = lax.broadcasted_iota(jnp.int32, (8, size_x), 0)
    for place in range(3 * rough_z):
        for tile in range(tiles):
            value = None
            for part in range(8 // up_y):
                at = place * 16 + tile * (8 // up_y) + part
                line = jnp.broadcast_to(wide_rows[at : at + 1], (8, size_x))
                value = line if value is None else jnp.where(wide_sub < part * up_y, value, line)
            force[place // rough_z, place % rough_z, tile * 8 : tile * 8 + 8] = value

    share = 1.0 - 0.5 / relax_time
    keep = 1.0 - 1.0 / relax_time

    def block(at, first, edge):
        rows = pl.ds(first, 8)
        out_rows = pl.ds(first + SIDE, 8)
        f = [popv[i, at, rows] for i in range(19)]
        kind = cells[at + 1, out_rows]
        half_force = [force[a, at // up_z if isinstance(at, int) else lax.div(at, up_z), rows] for a in range(3)]
        fluid = kind == 0
        wall = kind == 1
        inlet = kind == 2
        pairs = range(1, 19, 2)
        both = {i: f[i] + f[i + 1] for i in pairs}
        apart = {i: f[i] - f[i + 1] for i in pairs}
        density = f[0]
        mom = [None, None, None]
        for i in pairs:
            density = density + both[i]
            for a in range(3):
                step = lattice_dirs[i][a]
                if step != 0:
                    mom[a] = apart[i] if mom[a] is None else (
                        mom[a] + apart[i] if step > 0 else mom[a] - apart[i]
                    )
        inverse = 1.0 / density
        still = (0.0, 0.0, -inlet_speed)
        vel = [
            jnp.where(inlet, jnp.float32(still[a]), (mom[a] + half_force[a]) * inverse)
            for a in range(3)
        ]
        small = lattice_weights[-1]
        scale = jnp.where(fluid, density * (small / relax_time), jnp.where(wall, 0.0, small))
        kept_even = jnp.where(fluid, jnp.float32(0.5 * keep), jnp.where(wall, 0.5, 0.0))
        kept_odd = jnp.where(wall, jnp.float32(-0.5), kept_even)
        push = [jnp.where(fluid, (6.0 * share * small) * half_force[a], 0.0) for a in range(3)]
        vel15 = [1.5 * vel[a] for a in range(3)]
        square = vel15[0] * vel[0] + vel15[1] * vel[1] + vel15[2] * vel[2]
        work = vel[0] * push[0] + vel[1] * push[1] + vel[2] * push[2]
        base = scale - scale * square - work
        scale3 = 3.0 * scale
        line = [scale3 * vel[a] + push[a] for a in range(3)]
        line_more = [line[a] + push[a] for a in range(3)]
        result = [None] * 19
        result[0] = (2.0 * kept_even) * f[0] + 12.0 * base
        base2 = 2.0 * base
        for i in pairs:
            steps = lattice_dirs[i]
            along = signed_sum(steps, vel15)
            odd = signed_sum(steps, line)
            more = along * signed_sum(steps, line_more)
            if i < 7:
                odd = 2.0 * odd
                even = base2 + 2.0 * more
            else:
                even = base + more
            even = kept_even * both[i] + even
            odd = kept_odd * apart[i] + odd
            result[i] = even + odd
            result[i + 1] = even - odd
        for i in range(19):
            post[slot_of[i], at + 1, out_rows] = result[i]
        if edge != 0:
            side, pick = (0, 7) if edge > 0 else (1, 0)
            for k, i in enumerate(leaving_y[edge]):
                ysend[side, k, pl.ds(at, 1)] = result[i][pick : pick + 1]

    last = size_y - 8
    for load, at, out_z in ((0, size_z - 1, 1), (1, 0, -1)):
        loads[load].wait()
        block(at, 0, -1)
        for tile in range(1, tiles - 1):
            block(at, tile * 8, 0)
        block(at, last, 1)
        for number, way in enumerate(ways):
            if way[0] == out_z:
                start(post_copy, number)
    loads[2].wait()

    def sides(at, carry):
        block(at, 0, -1)
        block(at, last, 1)
        return carry

    lax.fori_loop(1, size_z - 1, sides, 0)
    for number, way in enumerate(ways):
        if way[0] == 0:
            start(post_copy, number)

    def middles(at, carry):
        for tile in range(1, tiles - 1):
            block(at, tile * 8, 0)
        return carry

    lax.fori_loop(1, size_z - 1, middles, 0)

    for number in range(8):
        wait_received(flag_copy, number)
    end_lane = lax.broadcasted_iota(jnp.int32, (rows_ext, size_x), 1)

    def opens(layer, carry):
        state = jnp.where(cells[layer] != 1, 1, 0)
        back = jnp.where(end_lane > 0, pltpu.roll(state, 1, 1), 0)
        ahead = jnp.where(end_lane < size_x - 1, pltpu.roll(state, size_x - 1, 1), 0)
        bits_x[...] = state + 2 * back + 4 * ahead
        near = bits_x[SIDE - 1 : SIDE - 1 + size_y], bits_x[SIDE + 1 : SIDE + 1 + size_y]
        bits_xy[layer] = bits_x[SIDE : SIDE + size_y] + 8 * near[0] + 64 * near[1]
        return carry

    lax.fori_loop(0, size_z + 2, opens, 0)

    def join(at, carry):
        here = bits_xy[at + 1]
        word = here + 512 * bits_xy[at] + 262144 * bits_xy[at + 2]
        words[at] = jnp.where((here & 1) != 0, word, 0)
        return carry

    lax.fori_loop(0, size_z, join, 0)

    for number in range(8):
        wait_received(post_copy, number)
    for way, row_at in ((1, SIDE - 1), (-1, SIDE + size_y)):
        side = 0 if way > 0 else 1
        for k, i in enumerate(leaving_y[way]):
            for layer in range(size_z):
                post[slot_of[i], layer + 1, row_at : row_at + 1] = yrecv[side, k, layer : layer + 1]

    for number in range(8):
        wait_sent(rough_copy, number)
        wait_sent(flag_copy, number)
        wait_sent(post_copy, number)


def bit_of(step_x, step_y, step_z):
    place = {0: 0, 1: 1, -1: 2}
    return 1 << (place[step_x] + 3 * place[step_y] + 9 * place[step_z])


def stream_kernel(post, words, pot_in, lor_in, out, pot_out, lor_out, held, sems, small_sems):
    size_z, size_y, size_x = words.shape
    own = pl.ds(SIDE, size_y)
    smalls = [
        pltpu.make_async_copy(pot_in, pot_out, small_sems.at[0]),
        pltpu.make_async_copy(lor_in, lor_out, small_sems.at[1]),
        pltpu.make_async_copy(
            post.at[slot_of[0], pl.ds(1, size_z), own], out.at[0], small_sems.at[2]
        ),
    ]
    for copy in smalls:
        copy.start()

    def store(at):
        return pltpu.make_async_copy(
            held.at[:, pl.ds(at, 1)], out.at[pl.ds(1, 18), pl.ds(at, 1)], sems.at[at]
        )

    def layer(at, carry):
        word = words[at]
        for i in range(1, 19):
            step_x, step_y, step_z = lattice_dirs[i]
            pulled = post[slot_of[i], at + 1 - step_z, pl.ds(SIDE - step_y, size_y)]
            if step_x != 0:
                pulled = pltpu.roll(pulled, step_x % size_x, 1)
            taken = (word & bit_of(step_x, step_y, step_z)) != 0
            held[i - 1, at] = jnp.where(taken, pulled, post[slot_of[opposite_dir[i]], at + 1, own])
        store(at).start()
        return carry

    lax.fori_loop(0, size_z, layer, 0)

    def finish(at, carry):
        store(at).wait()
        return carry

    lax.fori_loop(0, size_z, finish, 0)
    for copy in smalls:
        copy.wait()


def per_device(populations, flags, potential, conductivity, coil_phase, phase_table, magnetic):
    size_z, size_y, size_x = flags.shape
    rough_z, rough_y, rough_x = potential.shape
    assert rough_x * 2 <= 128 and rough_z >= REACH and 11 <= rough_y <= 13
    vmem = pl.BlockSpec(memory_space=pltpu.VMEM)
    hbm = pl.BlockSpec(memory_space=pltpu.HBM)
    ext = (size_z + 2, size_y + 2 * SIDE, size_x)
    f32, i32 = jnp.float32, jnp.int32
    post, words, potential_now, lorentz = pl.pallas_call(
        exchange_kernel,
        out_shape=(
            pltpu.VMEM((19,) + ext, f32),
            pltpu.VMEM(flags.shape, i32),
            pltpu.VMEM(potential.shape, f32),
            pltpu.VMEM(magnetic.shape, f32),
        ),
        in_specs=[hbm] * 7,
        out_specs=(vmem,) * 4,
        scratch_shapes=[
            pltpu.VMEM(populations.shape, f32),
            pltpu.VMEM(potential.shape, f32),
            pltpu.VMEM(potential.shape, f32),
            pltpu.VMEM(potential.shape, i32),
            pltpu.VMEM(magnetic.shape, f32),
            pltpu.VMEM(phase_table.shape, f32),
            pltpu.VMEM((rough_z, 16, 128), f32),
            pltpu.VMEM((8, rough_z, 16, 128), f32),
            pltpu.VMEM(ext, i32),
            pltpu.VMEM(ext[1:], i32),
            pltpu.VMEM((size_z + 2, size_y, size_x), i32),
            pltpu.VMEM((2, 5, -(-size_z // 8) * 8, size_x), f32),
            pltpu.VMEM((2, 5, -(-size_z // 8) * 8, size_x), f32),
            pltpu.VMEM((3 * rough_z, 16, 128), f32),
            pltpu.VMEM((3, rough_z, size_y, size_x), f32),
            pltpu.SemaphoreType.DMA((9,)),
        ]
        + [pltpu.SemaphoreType.DMA((8,))] * 6,
        compiler_params=pltpu.CompilerParams(
            collective_id=0, has_side_effects=True, vmem_limit_bytes=24 * 2**20
        ),
        name="exchange_and_collide",
    )(
        *(
            pltpu.with_memory_space_constraint(x, pltpu.HBM)
            for x in (
                populations, flags, potential, conductivity, coil_phase, magnetic, phase_table
            )
        )
    )
    result, potential_now, lorentz = pl.pallas_call(
        stream_kernel,
        out_shape=(
            jax.ShapeDtypeStruct(populations.shape, f32),
            jax.ShapeDtypeStruct(potential.shape, f32),
            jax.ShapeDtypeStruct(magnetic.shape, f32),
        ),
        in_specs=[vmem] * 4,
        out_specs=(hbm,) * 3,
        scratch_shapes=[
            pltpu.VMEM((18,) + flags.shape, f32),
            pltpu.SemaphoreType.DMA((size_z,)),
            pltpu.SemaphoreType.DMA((3,)),
        ],
        compiler_params=pltpu.CompilerParams(vmem_limit_bytes=24 * 2**20),
        name="stream",
    )(
        *(
            pltpu.with_memory_space_constraint(x, pltpu.VMEM)
            for x in (post, words, potential_now, lorentz)
        )
    )
    return (result, potential_now, lorentz)


def solution(mesh):
    in_specs = (
        P(None, ("groups", "wide"), "narrow", None),
        P(("groups", "wide"), "narrow", None),
        P(("groups", "wide"), "narrow", None),
        P(("groups", "wide"), "narrow", None),
        P(("groups", "wide"), "narrow", None),
        P(),
        P(None, ("groups", "wide"), "narrow", None),
    )
    out_specs = (
        P(None, ("groups", "wide"), "narrow", None),
        P(("groups", "wide"), "narrow", None),
        P(None, ("groups", "wide"), "narrow", None),
    )
    return jax.shard_map(
        per_device, mesh=mesh, in_specs=in_specs, out_specs=out_specs, check_vma=False
    )
```

```python
import functools

import jax
import jax.numpy as jnp
from jax import lax
from jax.experimental import pallas as pl
from jax.experimental.pallas import tpu as pltpu
from jax.sharding import PartitionSpec as P

SWEEPS = 2
REACH = 3
SIDE = 8

lattice_dirs = [
    (0, 0, 0),
    (1, 0, 0),
    (-1, 0, 0),
    (0, 1, 0),
    (0, -1, 0),
    (0, 0, 1),
    (0, 0, -1),
    (1, 1, 0),
    (-1, -1, 0),
    (1, -1, 0),
    (-1, 1, 0),
    (1, 0, 1),
    (-1, 0, -1),
    (1, 0, -1),
    (-1, 0, 1),
    (0, 1, 1),
    (0, -1, -1),
    (0, 1, -1),
    (0, -1, 1),
]
opposite_dir = [0, 2, 1, 4, 3, 6, 5, 8, 7, 10, 9, 12, 11, 14, 13, 16, 15, 18, 17]
lattice_weights = [1.0 / 3.0] + [1.0 / 18.0] * 6 + [1.0 / 36.0] * 12
relax_time = 0.8
force_scale = 0.02
inlet_speed = 0.05

flat = [i for i in range(19) if lattice_dirs[i][2] == 0]
rising = [i for i in range(19) if lattice_dirs[i][2] == 1]
sinking = [i for i in range(19) if lattice_dirs[i][2] == -1]
slot_of = {number: place for place, number in enumerate(flat + rising + sinking)}
leaving_y = {
    1: [i for i in range(19) if lattice_dirs[i][1] == 1],
    -1: [i for i in range(19) if lattice_dirs[i][1] == -1],
}
corner_of = {
    (dz, dy): [i for i in range(19) if lattice_dirs[i] == (0, dy, dz)][0]
    for dz in (-1, 1)
    for dy in (-1, 1)
}
ways = [(1, 0), (-1, 0), (0, 1), (0, -1), (1, 1), (1, -1), (-1, 1), (-1, -1)]


def plus(a, b):
    if a is None:
        return b
    if b is None:
        return a
    return a + b


def signed_sum(steps, parts):
    total = None
    for step, part in zip(steps, parts):
        if step != 0:
            total = plus(total, part if step > 0 else -part)
    return total


def exchange_kernel(
    pop_hbm, flags_hbm, pot_hbm, cond_hbm, coil_hbm, mag_hbm, table_hbm,
    post, words, pot_out, lor_out,
    popv, pot, cond, coil, mag, table, coarse, rim, cells, bits_x, bits_xy,
    ysend, yrecv, lor_rows, force,
    in_sems, coarse_send, coarse_recv, flag_send, flag_recv, post_send, post_recv,
):
    size_z, size_y, size_x = flags_hbm.shape
    rough_z, rough_y, rough_x = pot.shape
    tiles = size_y // 8
    up_z, up_y, up_x = size_z // rough_z, size_y // rough_y, size_x // rough_x
    at_z, at_y = lax.axis_index("wide"), lax.axis_index("narrow")
    num_z, num_y = lax.axis_size("wide"), lax.axis_size("narrow")

    def has(dz, dy):
        inside = None
        for step, place, count in ((dz, at_z, num_z), (dy, at_y, num_y)):
            if step != 0:
                this = place < count - 1 if step > 0 else place > 0
                inside = this if inside is None else jnp.logical_and(inside, this)
        return inside

    def target(dz, dy):
        return {"wide": at_z + dz, "narrow": at_y + dy}

    smalls = []
    for number, (src, dst) in enumerate(
        [(pot_hbm, pot), (cond_hbm, cond), (coil_hbm, coil), (table_hbm, table),
         (flags_hbm, cells.at[pl.ds(1, size_z), pl.ds(SIDE, size_y)]), (mag_hbm, mag)]
    ):
        copy = pltpu.make_async_copy(src, dst, in_sems.at[3 + number])
        copy.start()
        smalls.append(copy)
    loads = []
    spans = [(size_z - 1, 1), (0, 1), (1, size_z - 2)]
    for number, (first, count) in enumerate(spans):
        copy = pltpu.make_async_copy(
            pop_hbm.at[:, pl.ds(first, count)], popv.at[:, pl.ds(first, count)], in_sems.at[number]
        )
        copy.start()
        loads.append(copy)

    rim[...] = jnp.zeros(rim.shape, jnp.float32)
    rows_ext = cells.shape[1]
    for layer in (0, size_z + 1):
        cells[layer] = jnp.ones((rows_ext, size_x), jnp.int32)
    for first in (0, SIDE + size_y):
        cells[1 : size_z + 1, first : first + SIDE] = jnp.ones((size_z, SIDE, size_x), jnp.int32)

    barrier = pltpu.get_barrier_semaphore()
    for way in ways:
        @pl.when(has(*way))
        def _(way=way):
            pl.semaphore_signal(
                barrier, inc=1, device_id=target(*way), device_id_type=pl.DeviceIdType.MESH
            )

    coarse[...] = jnp.zeros(coarse.shape, jnp.float32)
    lor_rows[...] = jnp.zeros(lor_rows.shape, jnp.float32)

    for copy in smalls[:4]:
        copy.wait()

    def looked_up(column):
        phase = coil[...]
        summed = jnp.zeros(phase.shape, jnp.float32)
        for number in range(3):
            summed = summed + jnp.where(phase == number, table[number : number + 1, column : column + 1], jnp.float32(0.0))
        return summed

    lanes3 = lax.broadcasted_iota(jnp.int32, coarse.shape, 2)
    coarse[:, 0:rough_y, 0:rough_x] = cond[...] * looked_up(0)
    moved = pltpu.roll(coarse[...], rough_x, 2)
    coarse[:, 0:rough_y, 0:rough_x] = pot[...]
    coarse[...] = jnp.where(lanes3 < rough_x, coarse[...], moved)

    def rough_copy(number):
        dz, dy = ways[number]
        layers = {0: (0, rough_z), 1: (rough_z - 2, 2), -1: (0, 2)}[dz] if dy != 0 else (0, rough_z)
        rows = {0: (0, 16), 1: (8, 8), -1: (0, 8)}[dy]
        return pltpu.make_async_remote_copy(
            src_ref=coarse.at[pl.ds(*layers), pl.ds(*rows)],
            dst_ref=rim.at[number, pl.ds(*layers), pl.ds(0, rows[1])],
            send_sem=coarse_send.at[number],
            recv_sem=coarse_recv.at[number],
            device_id=target(dz, dy),
            device_id_type=pl.DeviceIdType.MESH,
        )

    def flag_copy(number):
        dz, dy = ways[number]
        src_z = {0: (0, size_z), 1: (size_z - 1, 1), -1: (0, 1)}[dz]
        dst_z = {0: 1, 1: 0, -1: size_z + 1}[dz]
        src_y = {0: (0, size_y), 1: (size_y - SIDE, SIDE), -1: (0, SIDE)}[dy]
        dst_y = {0: SIDE, 1: 0, -1: SIDE + size_y}[dy]
        return pltpu.make_async_remote_copy(
            src_ref=cells.at[pl.ds(src_z[0] + 1, src_z[1]), pl.ds(src_y[0] + SIDE, src_y[1])],
            dst_ref=cells.at[pl.ds(dst_z, src_z[1]), pl.ds(dst_y, src_y[1])],
            send_sem=flag_send.at[number],
            recv_sem=flag_recv.at[number],
            device_id=target(dz, dy),
            device_id_type=pl.DeviceIdType.MESH,
        )

    def post_copy(number):
        dz, dy = ways[number]
        if dz == 0:
            side = 0 if dy > 0 else 1
            src, dst = ysend.at[side], yrecv.at[side]
        else:
            src_layer = size_z if dz > 0 else 1
            dst_layer = 0 if dz > 0 else size_z + 1
            if dy == 0:
                group = rising if dz > 0 else sinking
                held = pl.ds(slot_of[group[0]], len(group))
                src = post.at[held, src_layer, pl.ds(SIDE, size_y)]
                dst = post.at[held, dst_layer, pl.ds(SIDE, size_y)]
            else:
                slot = slot_of[corner_of[(dz, dy)]]
                src_row, dst_row = (size_y, 0) if dy > 0 else (SIDE, SIDE + size_y)
                src = post.at[slot, src_layer, pl.ds(src_row, SIDE)]
                dst = post.at[slot, dst_layer, pl.ds(dst_row, SIDE)]
        return pltpu.make_async_remote_copy(
            src_ref=src,
            dst_ref=dst,
            send_sem=post_send.at[number],
            recv_sem=post_recv.at[number],
            device_id=target(dz, dy),
            device_id_type=pl.DeviceIdType.MESH,
        )

    def start(make, number):
        @pl.when(has(*ways[number]))
        def _():
            make(number).start()

    def wait_sent(make, number):
        @pl.when(has(*ways[number]))
        def _():
            make(number).wait_send()

    def wait_received(make, number):
        dz, dy = ways[number]

        @pl.when(has(-dz, -dy))
        def _():
            make(number).wait_recv()

    beside_z = (at_z > 0).astype(jnp.int32) + (at_z < num_z - 1).astype(jnp.int32)
    beside_y = (at_y > 0).astype(jnp.int32) + (at_y < num_y - 1).astype(jnp.int32)
    pl.semaphore_wait(barrier, (beside_z + 1) * (beside_y + 1) - 1)

    for number in range(8):
        start(rough_copy, number)
    smalls[4].wait()
    for number in range(8):
        start(flag_copy, number)
    smalls[5].wait()

    for number in range(8):
        wait_received(rough_copy, number)

    tall = 3 * 8
    row = lax.broadcasted_iota(jnp.int32, (tall, 128), 0)
    lane = lax.broadcasted_iota(jnp.int32, (tall, 128), 1)
    sub = lax.broadcasted_iota(jnp.int32, (8, 128), 0)
    row_all = at_y * rough_y + row - 8
    shown = (lane < rough_x) & (row_all >= 0) & (row_all < num_y * rough_y)
    blocks = {}
    number_of = {way: number for number, way in enumerate(ways)}
    gap = 16 - rough_y
    for dz in (-1, 0, 1):
        for layer in range(rough_z):
            if dz == 0:
                low, high = coarse[layer, 0:8], coarse[layer, 8:16]
            else:
                middle = number_of[(-dz, 0)]
                low, high = rim[middle, layer, 0:8], rim[middle, layer, 8:16]
            before = rim[number_of[(-dz, 1)], layer, 0:8]
            after = rim[number_of[(-dz, -1)], layer, 0:8]
            before = pltpu.roll(before, gap, 0)
            after = jnp.where(sub < rough_y - 8, high, pltpu.roll(after, rough_y - 8, 0))
            blocks[dz * rough_z + layer] = jnp.concatenate([before, low, after], axis=0)
    places = list(range(-REACH, rough_z + REACH))
    field = {p: jnp.where(shown, blocks[p], 0.0) for p in places}
    layer_all = {p: at_z * rough_z + p for p in places}

    def around(v):
        return (
            pltpu.roll(v, 1, 0), pltpu.roll(v, tall - 1, 0), pltpu.roll(v, 1, 1), pltpu.roll(v, 127, 1)
        )

    for sweep in range(SWEEPS):
        fresh = {}
        for p in places[sweep + 1 : len(places) - sweep - 1]:
            back_y, next_y, back_x, next_x = around(field[p])
            source = pltpu.roll(blocks[p], 128 - rough_x, 1)
            total = field[p + 1] + field[p - 1] + next_y + back_y + next_x + back_x + source
            inside = shown & (layer_all[p] >= 0) & (layer_all[p] < num_z * rough_z)
            fresh[p] = jnp.where(inside, total * jnp.float32(1.0 / 6.0), 0.0)
        field = fresh
    held_phase = [looked_up(1 + a) for a in range(3)]
    for layer in range(rough_z):
        back_y, next_y, back_x, next_x = around(field[layer])
        grads = (
            (next_x - back_x) * 0.5, (next_y - back_y) * 0.5, (field[layer + 1] - field[layer - 1]) * 0.5
        )
        pot_out[layer] = field[layer][8 : 8 + rough_y, 0:rough_x]
        cur = [
            cond[layer] * (held_phase[a][layer] - grads[a][8 : 8 + rough_y, 0:rough_x])
            for a in range(3)
        ]
        for a in range(3):
            b, c = (a + 1) % 3, (a + 2) % 3
            value = cur[b] * mag[c, layer] - cur[c] * mag[b, layer]
            lor_out[a, layer] = value
            lor_rows[a * rough_z + layer, 0:rough_y, 0:rough_x] = value

    wide_lane = lax.broadcasted_iota(jnp.int32, (8, size_x), 1)
    wide_sub = lax.broadcasted_iota(jnp.int32, (8, size_x), 0)
    from_lane = lax.div(wide_lane, jnp.full((8, size_x), up_x, jnp.int32))
    for place in range(3 * rough_z):
        spread = [
            jnp.take_along_axis(lor_rows[place, first : first + 8], from_lane, axis=1)
            * (0.5 * force_scale)
            for first in (0, 8)
        ]
        for tile in range(tiles):
            value = None
            for part in range(8 // up_y):
                at = tile * (8 // up_y) + part
                one = jnp.broadcast_to(spread[at // 8][at % 8 : at % 8 + 1], (8, size_x))
                value = one if value is None else jnp.where(wide_sub < part * up_y, value, one)
            force[place // rough_z, place % rough_z, tile * 8 : tile * 8 + 8] = value

    share = 1.0 - 0.5 / relax_time
    keep = 1.0 - 1.0 / relax_time

    def block(at, first, edge):
        rows = pl.ds(first, 8)
        out_rows = pl.ds(first + SIDE, 8)
        f = [popv[i, at, rows] for i in range(19)]
        kind = cells[at + 1, out_rows]
        half_force = [force[a, at // up_z if isinstance(at, int) else lax.div(at, up_z), rows] for a in range(3)]
        fluid = kind == 0
        wall = kind == 1
        inlet = kind == 2
        pairs = range(1, 19, 2)
        both = {i: f[i] + f[i + 1] for i in pairs}
        apart = {i: f[i] - f[i + 1] for i in pairs}
        density = f[0]
        mom = [None, None, None]
        for i in pairs:
            density = density + both[i]
            for a in range(3):
                step = lattice_dirs[i][a]
                if step != 0:
                    mom[a] = apart[i] if mom[a] is None else (
                        mom[a] + apart[i] if step > 0 else mom[a] - apart[i]
                    )
        inverse = 1.0 / density
        still = (0.0, 0.0, -inlet_speed)
        vel = [
            jnp.where(inlet, jnp.float32(still[a]), (mom[a] + half_force[a]) * inverse)
            for a in range(3)
        ]
        small = lattice_weights[-1]
        scale = jnp.where(fluid, density * (small / relax_time), jnp.where(wall, 0.0, small))
        kept_even = jnp.where(fluid, jnp.float32(0.5 * keep), jnp.where(wall, 0.5, 0.0))
        kept_odd = jnp.where(wall, jnp.float32(-0.5), kept_even)
        push = [jnp.where(fluid, (6.0 * share * small) * half_force[a], 0.0) for a in range(3)]
        vel15 = [1.5 * vel[a] for a in range(3)]
        square = vel15[0] * vel[0] + vel15[1] * vel[1] + vel15[2] * vel[2]
        work = vel[0] * push[0] + vel[1] * push[1] + vel[2] * push[2]
        base = scale - scale * square - work
        scale3 = 3.0 * scale
        line = [scale3 * vel[a] + push[a] for a in range(3)]
        line_more = [line[a] + push[a] for a in range(3)]
        result = [None] * 19
        result[0] = (2.0 * kept_even) * f[0] + 12.0 * base
        base2 = 2.0 * base
        for i in pairs:
            steps = lattice_dirs[i]
            along = signed_sum(steps, vel15)
            odd = signed_sum(steps, line)
            more = along * signed_sum(steps, line_more)
            if i < 7:
                odd = 2.0 * odd
                even = base2 + 2.0 * more
            else:
                even = base + more
            even = kept_even * both[i] + even
            odd = kept_odd * apart[i] + odd
            result[i] = even + odd
            result[i + 1] = even - odd
        for i in range(19):
            post[slot_of[i], at + 1, out_rows] = result[i]
        if edge != 0:
            side, pick = (0, 7) if edge > 0 else (1, 0)
            for k, i in enumerate(leaving_y[edge]):
                ysend[side, k, pl.ds(at, 1)] = result[i][pick : pick + 1]

    last = size_y - 8
    for load, at, out_z in ((0, size_z - 1, 1), (1, 0, -1)):
        loads[load].wait()
        block(at, 0, -1)
        for tile in range(1, tiles - 1):
            block(at, tile * 8, 0)
        block(at, last, 1)
        for number, way in enumerate(ways):
            if way[0] == out_z:
                start(post_copy, number)
    loads[2].wait()

    def sides(at, carry):
        block(at, 0, -1)
        block(at, last, 1)
        return carry

    lax.fori_loop(1, size_z - 1, sides, 0)
    for number, way in enumerate(ways):
        if way[0] == 0:
            start(post_copy, number)

    def middles(at, carry):
        for tile in range(1, tiles - 1):
            block(at, tile * 8, 0)
        return carry

    lax.fori_loop(1, size_z - 1, middles, 0)

    for number in range(8):
        wait_received(flag_copy, number)
    end_lane = lax.broadcasted_iota(jnp.int32, (rows_ext, size_x), 1)

    def opens(layer, carry):
        state = jnp.where(cells[layer] != 1, 1, 0)
        back = jnp.where(end_lane > 0, pltpu.roll(state, 1, 1), 0)
        ahead = jnp.where(end_lane < size_x - 1, pltpu.roll(state, size_x - 1, 1), 0)
        bits_x[...] = state + 2 * back + 4 * ahead
        near = bits_x[SIDE - 1 : SIDE - 1 + size_y], bits_x[SIDE + 1 : SIDE + 1 + size_y]
        bits_xy[layer] = bits_x[SIDE : SIDE + size_y] + 8 * near[0] + 64 * near[1]
        return carry

    lax.fori_loop(0, size_z + 2, opens, 0)

    def join(at, carry):
        here = bits_xy[at + 1]
        word = here + 512 * bits_xy[at] + 262144 * bits_xy[at + 2]
        words[at] = jnp.where((here & 1) != 0, word, 0)
        return carry

    lax.fori_loop(0, size_z, join, 0)

    for number in range(8):
        wait_received(post_copy, number)
    for way, row_at in ((1, SIDE - 1), (-1, SIDE + size_y)):
        side = 0 if way > 0 else 1
        for k, i in enumerate(leaving_y[way]):
            for layer in range(size_z):
                post[slot_of[i], layer + 1, row_at : row_at + 1] = yrecv[side, k, layer : layer + 1]

    for number in range(8):
        wait_sent(rough_copy, number)
        wait_sent(flag_copy, number)
        wait_sent(post_copy, number)


def bit_of(step_x, step_y, step_z):
    place = {0: 0, 1: 1, -1: 2}
    return 1 << (place[step_x] + 3 * place[step_y] + 9 * place[step_z])


def stream_kernel(post, words, pot_in, lor_in, out, pot_out, lor_out, held, sems, small_sems):
    size_z, size_y, size_x = words.shape
    own = pl.ds(SIDE, size_y)
    smalls = [
        pltpu.make_async_copy(pot_in, pot_out, small_sems.at[0]),
        pltpu.make_async_copy(lor_in, lor_out, small_sems.at[1]),
        pltpu.make_async_copy(
            post.at[slot_of[0], pl.ds(1, size_z), own], out.at[0], small_sems.at[2]
        ),
    ]
    for copy in smalls:
        copy.start()

    def store(at):
        return pltpu.make_async_copy(
            held.at[:, pl.ds(at, 1)], out.at[pl.ds(1, 18), pl.ds(at, 1)], sems.at[at]
        )

    def layer(at, carry):
        word = words[at]
        for i in range(1, 19):
            step_x, step_y, step_z = lattice_dirs[i]
            pulled = post[slot_of[i], at + 1 - step_z, pl.ds(SIDE - step_y, size_y)]
            if step_x != 0:
                pulled = pltpu.roll(pulled, step_x % size_x, 1)
            taken = (word & bit_of(step_x, step_y, step_z)) != 0
            held[i - 1, at] = jnp.where(taken, pulled, post[slot_of[opposite_dir[i]], at + 1, own])
        store(at).start()
        return carry

    lax.fori_loop(0, size_z, layer, 0)

    def finish(at, carry):
        store(at).wait()
        return carry

    lax.fori_loop(0, size_z, finish, 0)
    for copy in smalls:
        copy.wait()


def per_device(populations, flags, potential, conductivity, coil_phase, phase_table, magnetic):
    size_z, size_y, size_x = flags.shape
    rough_z, rough_y, rough_x = potential.shape
    assert rough_x * 2 <= 128 and rough_z >= REACH and 11 <= rough_y <= 13
    vmem = pl.BlockSpec(memory_space=pltpu.VMEM)
    hbm = pl.BlockSpec(memory_space=pltpu.HBM)
    ext = (size_z + 2, size_y + 2 * SIDE, size_x)
    f32, i32 = jnp.float32, jnp.int32
    post, words, potential_now, lorentz = pl.pallas_call(
        exchange_kernel,
        out_shape=(
            pltpu.VMEM((19,) + ext, f32),
            pltpu.VMEM(flags.shape, i32),
            pltpu.VMEM(potential.shape, f32),
            pltpu.VMEM(magnetic.shape, f32),
        ),
        in_specs=[hbm] * 7,
        out_specs=(vmem,) * 4,
        scratch_shapes=[
            pltpu.VMEM(populations.shape, f32),
            pltpu.VMEM(potential.shape, f32),
            pltpu.VMEM(potential.shape, f32),
            pltpu.VMEM(potential.shape, i32),
            pltpu.VMEM(magnetic.shape, f32),
            pltpu.VMEM(phase_table.shape, f32),
            pltpu.VMEM((rough_z, 16, 128), f32),
            pltpu.VMEM((8, rough_z, 16, 128), f32),
            pltpu.VMEM(ext, i32),
            pltpu.VMEM(ext[1:], i32),
            pltpu.VMEM((size_z + 2, size_y, size_x), i32),
            pltpu.VMEM((2, 5, -(-size_z // 8) * 8, size_x), f32),
            pltpu.VMEM((2, 5, -(-size_z // 8) * 8, size_x), f32),
            pltpu.VMEM((3 * rough_z, 16, 128), f32),
            pltpu.VMEM((3, rough_z, size_y, size_x), f32),
            pltpu.SemaphoreType.DMA((9,)),
        ]
        + [pltpu.SemaphoreType.DMA((8,))] * 6,
        compiler_params=pltpu.CompilerParams(
            collective_id=0, has_side_effects=True, vmem_limit_bytes=24 * 2**20
        ),
        name="exchange_and_collide",
    )(
        *(
            pltpu.with_memory_space_constraint(x, pltpu.HBM)
            for x in (
                populations, flags, potential, conductivity, coil_phase, magnetic, phase_table
            )
        )
    )
    result, potential_now, lorentz = pl.pallas_call(
        stream_kernel,
        out_shape=(
            jax.ShapeDtypeStruct(populations.shape, f32),
            jax.ShapeDtypeStruct(potential.shape, f32),
            jax.ShapeDtypeStruct(magnetic.shape, f32),
        ),
        in_specs=[vmem] * 4,
        out_specs=(hbm,) * 3,
        scratch_shapes=[
            pltpu.VMEM((18,) + flags.shape, f32),
            pltpu.SemaphoreType.DMA((size_z,)),
            pltpu.SemaphoreType.DMA((3,)),
        ],
        compiler_params=pltpu.CompilerParams(vmem_limit_bytes=24 * 2**20),
        name="stream",
    )(
        *(
            pltpu.with_memory_space_constraint(x, pltpu.VMEM)
            for x in (post, words, potential_now, lorentz)
        )
    )
    return (result, potential_now, lorentz)


def solution(mesh):
    in_specs = (
        P(None, ("groups", "wide"), "narrow", None),
        P(("groups", "wide"), "narrow", None),
        P(("groups", "wide"), "narrow", None),
        P(("groups", "wide"), "narrow", None),
        P(("groups", "wide"), "narrow", None),
        P(),
        P(None, ("groups", "wide"), "narrow", None),
    )
    out_specs = (
        P(None, ("groups", "wide"), "narrow", None),
        P(("groups", "wide"), "narrow", None),
        P(None, ("groups", "wide"), "narrow", None),
    )
    return jax.shard_map(
        per_device, mesh=mesh, in_specs=in_specs, out_specs=out_specs, check_vma=False
    )
```

```python
import functools

import jax
import jax.numpy as jnp
from jax import lax
from jax.experimental import pallas as pl
from jax.experimental.pallas import tpu as pltpu
from jax.sharding import PartitionSpec as P

SWEEPS = 2
REACH = 3
SIDE = 8

lattice_dirs = [
    (0, 0, 0),
    (1, 0, 0),
    (-1, 0, 0),
    (0, 1, 0),
    (0, -1, 0),
    (0, 0, 1),
    (0, 0, -1),
    (1, 1, 0),
    (-1, -1, 0),
    (1, -1, 0),
    (-1, 1, 0),
    (1, 0, 1),
    (-1, 0, -1),
    (1, 0, -1),
    (-1, 0, 1),
    (0, 1, 1),
    (0, -1, -1),
    (0, 1, -1),
    (0, -1, 1),
]
opposite_dir = [0, 2, 1, 4, 3, 6, 5, 8, 7, 10, 9, 12, 11, 14, 13, 16, 15, 18, 17]
lattice_weights = [1.0 / 3.0] + [1.0 / 18.0] * 6 + [1.0 / 36.0] * 12
relax_time = 0.8
force_scale = 0.02
inlet_speed = 0.05

flat = [i for i in range(19) if lattice_dirs[i][2] == 0]
rising = [i for i in range(19) if lattice_dirs[i][2] == 1]
sinking = [i for i in range(19) if lattice_dirs[i][2] == -1]
slot_of = {number: place for place, number in enumerate(flat + rising + sinking)}
leaving_y = {
    1: [i for i in range(19) if lattice_dirs[i][1] == 1],
    -1: [i for i in range(19) if lattice_dirs[i][1] == -1],
}
corner_of = {
    (dz, dy): [i for i in range(19) if lattice_dirs[i] == (0, dy, dz)][0]
    for dz in (-1, 1)
    for dy in (-1, 1)
}
ways = [(1, 0), (-1, 0), (0, 1), (0, -1), (1, 1), (1, -1), (-1, 1), (-1, -1)]


def plus(a, b):
    if a is None:
        return b
    if b is None:
        return a
    return a + b


def signed_sum(steps, parts):
    total = None
    for step, part in zip(steps, parts):
        if step != 0:
            total = plus(total, part if step > 0 else -part)
    return total


def exchange_kernel(
    pop_hbm, flags_hbm, pot_hbm, cond_hbm, coil_hbm, mag_hbm, table_hbm,
    post, words, pot_out, lor_out,
    popv, pot, cond, coil, mag, table, coarse, rim, cells, bits_x, bits_xy,
    ysend, yrecv, lor_rows, force,
    in_sems, coarse_send, coarse_recv, flag_send, flag_recv, post_send, post_recv,
):
    size_z, size_y, size_x = flags_hbm.shape
    rough_z, rough_y, rough_x = pot.shape
    tiles = size_y // 8
    up_z, up_y, up_x = size_z // rough_z, size_y // rough_y, size_x // rough_x
    at_z, at_y = lax.axis_index("wide"), lax.axis_index("narrow")
    num_z, num_y = lax.axis_size("wide"), lax.axis_size("narrow")

    def has(dz, dy):
        inside = None
        for step, place, count in ((dz, at_z, num_z), (dy, at_y, num_y)):
            if step != 0:
                this = place < count - 1 if step > 0 else place > 0
                inside = this if inside is None else jnp.logical_and(inside, this)
        return inside

    def target(dz, dy):
        return {"wide": at_z + dz, "narrow": at_y + dy}

    smalls = []
    for number, (src, dst) in enumerate(
        [(pot_hbm, pot), (cond_hbm, cond), (coil_hbm, coil), (table_hbm, table),
         (flags_hbm, cells.at[pl.ds(1, size_z), pl.ds(SIDE, size_y)]), (mag_hbm, mag)]
    ):
        copy = pltpu.make_async_copy(src, dst, in_sems.at[3 + number])
        copy.start()
        smalls.append(copy)
    loads = []
    spans = [(size_z - 1, 1), (0, 1), (1, size_z - 2)]
    for number, (first, count) in enumerate(spans):
        copy = pltpu.make_async_copy(
            pop_hbm.at[:, pl.ds(first, count)], popv.at[:, pl.ds(first, count)], in_sems.at[number]
        )
        copy.start()
        loads.append(copy)

    rim[...] = jnp.zeros(rim.shape, jnp.float32)
    rows_ext = cells.shape[1]
    for layer in (0, size_z + 1):
        cells[layer] = jnp.ones((rows_ext, size_x), jnp.int32)
    for first in (0, SIDE + size_y):
        cells[1 : size_z + 1, first : first + SIDE] = jnp.ones((size_z, SIDE, size_x), jnp.int32)

    barrier = pltpu.get_barrier_semaphore()
    for way in ways:
        @pl.when(has(*way))
        def _(way=way):
            pl.semaphore_signal(
                barrier, inc=1, device_id=target(*way), device_id_type=pl.DeviceIdType.MESH
            )

    coarse[...] = jnp.zeros(coarse.shape, jnp.float32)
    lor_rows[...] = jnp.zeros(lor_rows.shape, jnp.float32)

    for copy in smalls[:4]:
        copy.wait()

    def looked_up(column):
        phase = coil[...]
        summed = jnp.zeros(phase.shape, jnp.float32)
        for number in range(3):
            summed = summed + jnp.where(phase == number, table[number : number + 1, column : column + 1], jnp.float32(0.0))
        return summed

    lanes3 = lax.broadcasted_iota(jnp.int32, coarse.shape, 2)
    coarse[:, 0:rough_y, 0:rough_x] = cond[...] * looked_up(0)
    moved = pltpu.roll(coarse[...], rough_x, 2)
    coarse[:, 0:rough_y, 0:rough_x] = pot[...]
    coarse[...] = jnp.where(lanes3 < rough_x, coarse[...], moved)

    def rough_copy(number):
        dz, dy = ways[number]
        layers = {0: (0, rough_z), 1: (rough_z - 2, 2), -1: (0, 2)}[dz] if dy != 0 else (0, rough_z)
        rows = {0: (0, 16), 1: (8, 8), -1: (0, 8)}[dy]
        return pltpu.make_async_remote_copy(
            src_ref=coarse.at[pl.ds(*layers), pl.ds(*rows)],
            dst_ref=rim.at[number, pl.ds(*layers), pl.ds(0, rows[1])],
            send_sem=coarse_send.at[number],
            recv_sem=coarse_recv.at[number],
            device_id=target(dz, dy),
            device_id_type=pl.DeviceIdType.MESH,
        )

    def flag_copy(number):
        dz, dy = ways[number]
        src_z = {0: (0, size_z), 1: (size_z - 1, 1), -1: (0, 1)}[dz]
        dst_z = {0: 1, 1: 0, -1: size_z + 1}[dz]
        src_y = {0: (0, size_y), 1: (size_y - SIDE, SIDE), -1: (0, SIDE)}[dy]
        dst_y = {0: SIDE, 1: 0, -1: SIDE + size_y}[dy]
        return pltpu.make_async_remote_copy(
            src_ref=cells.at[pl.ds(src_z[0] + 1, src_z[1]), pl.ds(src_y[0] + SIDE, src_y[1])],
            dst_ref=cells.at[pl.ds(dst_z, src_z[1]), pl.ds(dst_y, src_y[1])],
            send_sem=flag_send.at[number],
            recv_sem=flag_recv.at[number],
            device_id=target(dz, dy),
            device_id_type=pl.DeviceIdType.MESH,
        )

    def post_copy(number):
        dz, dy = ways[number]
        if dz == 0:
            side = 0 if dy > 0 else 1
            src, dst = ysend.at[side], yrecv.at[side]
        else:
            src_layer = size_z if dz > 0 else 1
            dst_layer = 0 if dz > 0 else size_z + 1
            if dy == 0:
                group = rising if dz > 0 else sinking
                held = pl.ds(slot_of[group[0]], len(group))
                src = post.at[held, src_layer, pl.ds(SIDE, size_y)]
                dst = post.at[held, dst_layer, pl.ds(SIDE, size_y)]
            else:
                slot = slot_of[corner_of[(dz, dy)]]
                src_row, dst_row = (size_y, 0) if dy > 0 else (SIDE, SIDE + size_y)
                src = post.at[slot, src_layer, pl.ds(src_row, SIDE)]
                dst = post.at[slot, dst_layer, pl.ds(dst_row, SIDE)]
        return pltpu.make_async_remote_copy(
            src_ref=src,
            dst_ref=dst,
            send_sem=post_send.at[number],
            recv_sem=post_recv.at[number],
            device_id=target(dz, dy),
            device_id_type=pl.DeviceIdType.MESH,
        )

    def start(make, number):
        @pl.when(has(*ways[number]))
        def _():
            make(number).start()

    def wait_sent(make, number):
        @pl.when(has(*ways[number]))
        def _():
            make(number).wait_send()

    def wait_received(make, number):
        dz, dy = ways[number]

        @pl.when(has(-dz, -dy))
        def _():
            make(number).wait_recv()

    beside_z = (at_z > 0).astype(jnp.int32) + (at_z < num_z - 1).astype(jnp.int32)
    beside_y = (at_y > 0).astype(jnp.int32) + (at_y < num_y - 1).astype(jnp.int32)
    pl.semaphore_wait(barrier, (beside_z + 1) * (beside_y + 1) - 1)

    for number in range(8):
        start(rough_copy, number)

    smalls[4].wait()
    smalls[5].wait()
    for number in range(8):
        wait_received(rough_copy, number)
    for number in range(8):
        start(flag_copy, number)

    tall = 3 * 8
    row = lax.broadcasted_iota(jnp.int32, (tall, 128), 0)
    lane = lax.broadcasted_iota(jnp.int32, (tall, 128), 1)
    sub = lax.broadcasted_iota(jnp.int32, (8, 128), 0)
    row_all = at_y * rough_y + row - 8
    shown = (lane < rough_x) & (row_all >= 0) & (row_all < num_y * rough_y)
    blocks = {}
    number_of = {way: number for number, way in enumerate(ways)}
    gap = 16 - rough_y
    for dz in (-1, 0, 1):
        for layer in range(rough_z):
            if dz == 0:
                low, high = coarse[layer, 0:8], coarse[layer, 8:16]
            else:
                middle = number_of[(-dz, 0)]
                low, high = rim[middle, layer, 0:8], rim[middle, layer, 8:16]
            before = rim[number_of[(-dz, 1)], layer, 0:8]
            after = rim[number_of[(-dz, -1)], layer, 0:8]
            before = pltpu.roll(before, gap, 0)
            after = jnp.where(sub < rough_y - 8, high, pltpu.roll(after, rough_y - 8, 0))
            blocks[dz * rough_z + layer] = jnp.concatenate([before, low, after], axis=0)
    places = list(range(-REACH, rough_z + REACH))
    field = {p: jnp.where(shown, blocks[p], 0.0) for p in places}
    layer_all = {p: at_z * rough_z + p for p in places}

    def around(v):
        return (
            pltpu.roll(v, 1, 0), pltpu.roll(v, tall - 1, 0), pltpu.roll(v, 1, 1), pltpu.roll(v, 127, 1)
        )

    for sweep in range(SWEEPS):
        fresh = {}
        for p in places[sweep + 1 : len(places) - sweep - 1]:
            back_y, next_y, back_x, next_x = around(field[p])
            source = pltpu.roll(blocks[p], 128 - rough_x, 1)
            total = field[p + 1] + field[p - 1] + next_y + back_y + next_x + back_x + source
            inside = shown & (layer_all[p] >= 0) & (layer_all[p] < num_z * rough_z)
            fresh[p] = jnp.where(inside, total * jnp.float32(1.0 / 6.0), 0.0)
        field = fresh
    held_phase = [looked_up(1 + a) for a in range(3)]
    for layer in range(rough_z):
        back_y, next_y, back_x, next_x = around(field[layer])
        grads = (
            (next_x - back_x) * 0.5, (next_y - back_y) * 0.5, (field[layer + 1] - field[layer - 1]) * 0.5
        )
        pot_out[layer] = field[layer][8 : 8 + rough_y, 0:rough_x]
        cur = [
            cond[layer] * (held_phase[a][layer] - grads[a][8 : 8 + rough_y, 0:rough_x])
            for a in range(3)
        ]
        for a in range(3):
            b, c = (a + 1) % 3, (a + 2) % 3
            value = cur[b] * mag[c, layer] - cur[c] * mag[b, layer]
            lor_out[a, layer] = value
            lor_rows[a * rough_z + layer, 0:rough_y, 0:rough_x] = value

    wide_lane = lax.broadcasted_iota(jnp.int32, (8, size_x), 1)
    wide_sub = lax.broadcasted_iota(jnp.int32, (8, size_x), 0)
    from_lane = lax.div(wide_lane, jnp.full((8, size_x), up_x, jnp.int32))
    for place in range(3 * rough_z):
        spread = [
            jnp.take_along_axis(lor_rows[place, first : first + 8], from_lane, axis=1)
            * (0.5 * force_scale)
            for first in (0, 8)
        ]
        for tile in range(tiles):
            value = None
            for part in range(8 // up_y):
                at = tile * (8 // up_y) + part
                one = jnp.broadcast_to(spread[at // 8][at % 8 : at % 8 + 1], (8, size_x))
                value = one if value is None else jnp.where(wide_sub < part * up_y, value, one)
            force[place // rough_z, place % rough_z, tile * 8 : tile * 8 + 8] = value

    share = 1.0 - 0.5 / relax_time
    keep = 1.0 - 1.0 / relax_time

    def block(at, first, edge):
        rows = pl.ds(first, 8)
        out_rows = pl.ds(first + SIDE, 8)
        f = [popv[i, at, rows] for i in range(19)]
        kind = cells[at + 1, out_rows]
        half_force = [force[a, at // up_z if isinstance(at, int) else lax.div(at, up_z), rows] for a in range(3)]
        fluid = kind == 0
        wall = kind == 1
        inlet = kind == 2
        pairs = range(1, 19, 2)
        both = {i: f[i] + f[i + 1] for i in pairs}
        apart = {i: f[i] - f[i + 1] for i in pairs}
        density = f[0]
        mom = [None, None, None]
        for i in pairs:
            density = density + both[i]
            for a in range(3):
                step = lattice_dirs[i][a]
                if step != 0:
                    mom[a] = apart[i] if mom[a] is None else (
                        mom[a] + apart[i] if step > 0 else mom[a] - apart[i]
                    )
        inverse = 1.0 / density
        still = (0.0, 0.0, -inlet_speed)
        vel = [
            jnp.where(inlet, jnp.float32(still[a]), (mom[a] + half_force[a]) * inverse)
            for a in range(3)
        ]
        small = lattice_weights[-1]
        scale = jnp.where(fluid, density * (small / relax_time), jnp.where(wall, 0.0, small))
        kept_even = jnp.where(fluid, jnp.float32(0.5 * keep), jnp.where(wall, 0.5, 0.0))
        kept_odd = jnp.where(wall, jnp.float32(-0.5), kept_even)
        push = [jnp.where(fluid, (6.0 * share * small) * half_force[a], 0.0) for a in range(3)]
        vel15 = [1.5 * vel[a] for a in range(3)]
        square = vel15[0] * vel[0] + vel15[1] * vel[1] + vel15[2] * vel[2]
        work = vel[0] * push[0] + vel[1] * push[1] + vel[2] * push[2]
        base = scale - scale * square - work
        scale3 = 3.0 * scale
        line = [scale3 * vel[a] + push[a] for a in range(3)]
        line_more = [line[a] + push[a] for a in range(3)]
        result = [None] * 19
        result[0] = (2.0 * kept_even) * f[0] + 12.0 * base
        base2 = 2.0 * base
        for i in pairs:
            steps = lattice_dirs[i]
            along = signed_sum(steps, vel15)
            odd = signed_sum(steps, line)
            more = along * signed_sum(steps, line_more)
            if i < 7:
                odd = 2.0 * odd
                even = base2 + 2.0 * more
            else:
                even = base + more
            even = kept_even * both[i] + even
            odd = kept_odd * apart[i] + odd
            result[i] = even + odd
            result[i + 1] = even - odd
        for i in range(19):
            post[slot_of[i], at + 1, out_rows] = result[i]
        if edge != 0:
            side, pick = (0, 7) if edge > 0 else (1, 0)
            for k, i in enumerate(leaving_y[edge]):
                ysend[side, k, pl.ds(at, 1)] = result[i][pick : pick + 1]

    last = size_y - 8
    for load, at, out_z in ((0, size_z - 1, 1), (1, 0, -1)):
        loads[load].wait()
        block(at, 0, -1)
        for tile in range(1, tiles - 1):
            block(at, tile * 8, 0)
        block(at, last, 1)
        for number, way in enumerate(ways):
            if way[0] == out_z:
                start(post_copy, number)
    loads[2].wait()

    def sides(at, carry):
        block(at, 0, -1)
        block(at, last, 1)
        return carry

    lax.fori_loop(1, size_z - 1, sides, 0)
    for number, way in enumerate(ways):
        if way[0] == 0:
            start(post_copy, number)

    def middles(at, carry):
        for tile in range(1, tiles - 1):
            block(at, tile * 8, 0)
        return carry

    lax.fori_loop(1, size_z - 1, middles, 0)

    for number in range(8):
        wait_received(flag_copy, number)
    end_lane = lax.broadcasted_iota(jnp.int32, (rows_ext, size_x), 1)

    def opens(layer, carry):
        state = jnp.where(cells[layer] != 1, 1, 0)
        back = jnp.where(end_lane > 0, pltpu.roll(state, 1, 1), 0)
        ahead = jnp.where(end_lane < size_x - 1, pltpu.roll(state, size_x - 1, 1), 0)
        bits_x[...] = state + 2 * back + 4 * ahead
        near = bits_x[SIDE - 1 : SIDE - 1 + size_y], bits_x[SIDE + 1 : SIDE + 1 + size_y]
        bits_xy[layer] = bits_x[SIDE : SIDE + size_y] + 8 * near[0] + 64 * near[1]
        return carry

    lax.fori_loop(0, size_z + 2, opens, 0)

    def join(at, carry):
        here = bits_xy[at + 1]
        word = here + 512 * bits_xy[at] + 262144 * bits_xy[at + 2]
        words[at] = jnp.where((here & 1) != 0, word, 0)
        return carry

    lax.fori_loop(0, size_z, join, 0)

    for number in (2, 3):
        wait_received(post_copy, number)
    for way, row_at in ((1, SIDE - 1), (-1, SIDE + size_y)):
        side = 0 if way > 0 else 1
        for k, i in enumerate(leaving_y[way]):
            for layer in range(size_z):
                post[slot_of[i], layer + 1, row_at : row_at + 1] = yrecv[side, k, layer : layer + 1]

    for number in range(8):
        wait_sent(rough_copy, number)
        wait_sent(flag_copy, number)
    for number in (0, 1, 4, 5, 6, 7):
        wait_received(post_copy, number)
    for number in range(8):
        wait_sent(post_copy, number)


def bit_of(step_x, step_y, step_z):
    place = {0: 0, 1: 1, -1: 2}
    return 1 << (place[step_x] + 3 * place[step_y] + 9 * place[step_z])


def stream_kernel(post, words, pot_in, lor_in, out, pot_out, lor_out, held, sems, small_sems):
    size_z, size_y, size_x = words.shape
    own = pl.ds(SIDE, size_y)
    smalls = [
        pltpu.make_async_copy(pot_in, pot_out, small_sems.at[0]),
        pltpu.make_async_copy(lor_in, lor_out, small_sems.at[1]),
        pltpu.make_async_copy(
            post.at[slot_of[0], pl.ds(1, size_z), own], out.at[0], small_sems.at[2]
        ),
    ]
    for copy in smalls:
        copy.start()

    def store(at):
        return pltpu.make_async_copy(
            held.at[:, pl.ds(at, 1)], out.at[pl.ds(1, 18), pl.ds(at, 1)], sems.at[at]
        )

    def layer(at, carry):
        word = words[at]
        for i in range(1, 19):
            step_x, step_y, step_z = lattice_dirs[i]
            pulled = post[slot_of[i], at + 1 - step_z, pl.ds(SIDE - step_y, size_y)]
            if step_x != 0:
                pulled = pltpu.roll(pulled, step_x % size_x, 1)
            taken = (word & bit_of(step_x, step_y, step_z)) != 0
            held[i - 1, at] = jnp.where(taken, pulled, post[slot_of[opposite_dir[i]], at + 1, own])
        store(at).start()
        return carry

    lax.fori_loop(0, size_z, layer, 0)

    def finish(at, carry):
        store(at).wait()
        return carry

    lax.fori_loop(0, size_z, finish, 0)
    for copy in smalls:
        copy.wait()


def per_device(populations, flags, potential, conductivity, coil_phase, phase_table, magnetic):
    size_z, size_y, size_x = flags.shape
    rough_z, rough_y, rough_x = potential.shape
    assert rough_x * 2 <= 128 and rough_z >= REACH and 11 <= rough_y <= 13
    vmem = pl.BlockSpec(memory_space=pltpu.VMEM)
    hbm = pl.BlockSpec(memory_space=pltpu.HBM)
    ext = (size_z + 2, size_y + 2 * SIDE, size_x)
    f32, i32 = jnp.float32, jnp.int32
    post, words, potential_now, lorentz = pl.pallas_call(
        exchange_kernel,
        out_shape=(
            pltpu.VMEM((19,) + ext, f32),
            pltpu.VMEM(flags.shape, i32),
            pltpu.VMEM(potential.shape, f32),
            pltpu.VMEM(magnetic.shape, f32),
        ),
        in_specs=[hbm] * 7,
        out_specs=(vmem,) * 4,
        scratch_shapes=[
            pltpu.VMEM(populations.shape, f32),
            pltpu.VMEM(potential.shape, f32),
            pltpu.VMEM(potential.shape, f32),
            pltpu.VMEM(potential.shape, i32),
            pltpu.VMEM(magnetic.shape, f32),
            pltpu.VMEM(phase_table.shape, f32),
            pltpu.VMEM((rough_z, 16, 128), f32),
            pltpu.VMEM((8, rough_z, 16, 128), f32),
            pltpu.VMEM(ext, i32),
            pltpu.VMEM(ext[1:], i32),
            pltpu.VMEM((size_z + 2, size_y, size_x), i32),
            pltpu.VMEM((2, 5, -(-size_z // 8) * 8, size_x), f32),
            pltpu.VMEM((2, 5, -(-size_z // 8) * 8, size_x), f32),
            pltpu.VMEM((3 * rough_z, 16, 128), f32),
            pltpu.VMEM((3, rough_z, size_y, size_x), f32),
            pltpu.SemaphoreType.DMA((9,)),
        ]
        + [pltpu.SemaphoreType.DMA((8,))] * 6,
        compiler_params=pltpu.CompilerParams(
            collective_id=0, has_side_effects=True, vmem_limit_bytes=24 * 2**20
        ),
        name="exchange_and_collide",
    )(
        *(
            pltpu.with_memory_space_constraint(x, pltpu.HBM)
            for x in (
                populations, flags, potential, conductivity, coil_phase, magnetic, phase_table
            )
        )
    )
    result, potential_now, lorentz = pl.pallas_call(
        stream_kernel,
        out_shape=(
            jax.ShapeDtypeStruct(populations.shape, f32),
            jax.ShapeDtypeStruct(potential.shape, f32),
            jax.ShapeDtypeStruct(magnetic.shape, f32),
        ),
        in_specs=[vmem] * 4,
        out_specs=(hbm,) * 3,
        scratch_shapes=[
            pltpu.VMEM((18,) + flags.shape, f32),
            pltpu.SemaphoreType.DMA((size_z,)),
            pltpu.SemaphoreType.DMA((3,)),
        ],
        compiler_params=pltpu.CompilerParams(vmem_limit_bytes=24 * 2**20),
        name="stream",
    )(
        *(
            pltpu.with_memory_space_constraint(x, pltpu.VMEM)
            for x in (post, words, potential_now, lorentz)
        )
    )
    return (result, potential_now, lorentz)


def solution(mesh):
    in_specs = (
        P(None, ("groups", "wide"), "narrow", None),
        P(("groups", "wide"), "narrow", None),
        P(("groups", "wide"), "narrow", None),
        P(("groups", "wide"), "narrow", None),
        P(("groups", "wide"), "narrow", None),
        P(),
        P(None, ("groups", "wide"), "narrow", None),
    )
    out_specs = (
        P(None, ("groups", "wide"), "narrow", None),
        P(("groups", "wide"), "narrow", None),
        P(None, ("groups", "wide"), "narrow", None),
    )
    return jax.shard_map(
        per_device, mesh=mesh, in_specs=in_specs, out_specs=out_specs, check_vma=False
    )
```
